128 devices in a mesh: ctx: 32 (over x, y, core), head: 4 (over z).
Axes of the slice: x: 4, y: 4, z: 4, core: 2. Of those that a mesh axis runs over, the one named last changes fastest.
Arguments:
- queries: bfloat16 [24576, 2048], P(('ctx', 'head')), may hold values from -9 to 9
- keys: bfloat16 [24576, 2048], P(('ctx', 'head')), may hold values from -9 to 9
- values: bfloat16 [24576, 2048], P(('ctx', 'head')), may hold values from -12 to 12
- grad_out: bfloat16 [24576, 2048], P(('ctx', 'head')), may hold values from -6 to 6
- pattern: int32 [192, 16], replicated, may hold values from -1 to 191, as said below
Outputs:
- attn_out: bfloat16 [24576, 2048], P(('ctx', 'head'))
- grad_query: bfloat16 [24576, 2048], P(('ctx', 'head'))
- grad_key: bfloat16 [24576, 2048], P(('ctx', 'head'))
- grad_value: bfloat16 [24576, 2048], P(('ctx', 'head'))
The draws below stay inside these ranges and needn't reach their ends.
Inputs may be any that keep to these rules, and one draw needn't show every extreme that they name: `pattern`: row b: entries 0 to 3 are the blocks b - 3 to b in order, -1 where such a number is negative; the remaining entries are, ascending, some of the blocks c <= b - 4 whose remainder modulo 16 equals one phase shared by all rows (each row its own subset, always holding the smallest such block where one exists), followed by -1.
All inputs are finite; a program needn't handle non-finite values.
Results may differ from the reference program's by a relative error of at most 0.015.
Values may be sent and summed in bfloat16 or wider, within the bound.
A program may use at most 128 MiB of HBM per device.

```python
import math
import jax
import jax.numpy as jnp
from jax import lax

HEAD_DIM = 128
BLOCK = 128
LOCAL = 4
STRIDE = 16
HEADS = 16
TOKENS = 24576
NBLOCKS = 192
SLOTS = 16


def base_field(key, label):
    raw = jax.random.normal(jax.random.fold_in(key, label), (TOKENS, HEADS * HEAD_DIM), jnp.float32)
    return jnp.clip(1.5 * raw, -9.0, 9.0)


def draw_queries(key, part):
    field = base_field(key, 1)
    return field.astype(jnp.bfloat16)


def draw_keys(key, part):
    field = base_field(key, 2)
    return field.astype(jnp.bfloat16)


def draw_pattern(key, part):
    stride_phase = jax.random.randint(jax.random.fold_in(key, 5), (), 0, STRIDE)
    block_rows = jnp.arange(NBLOCKS, dtype=jnp.int32)[:, None]
    near_blocks = block_rows - (LOCAL - 1) + jnp.arange(LOCAL, dtype=jnp.int32)[None, :]
    near_blocks = jnp.where(near_blocks >= 0, near_blocks, -1)
    far_count = NBLOCKS // STRIDE
    far_index = jnp.arange(far_count, dtype=jnp.int32)[None, :]
    far_blocks = stride_phase + STRIDE * far_index
    eligible = far_blocks <= block_rows - LOCAL
    coins = jax.random.randint(jax.random.fold_in(key, 6), (NBLOCKS, far_count), 0, 4)
    keep_far = eligible & ((coins > 0) | (far_index == 0))
    ordered = jnp.sort(jnp.where(keep_far, far_blocks, NBLOCKS + far_blocks), axis=1)
    ordered = jnp.where(ordered < NBLOCKS, ordered, -1)
    return jnp.concatenate([near_blocks, ordered], axis=1).astype(jnp.int32)


def steps_of(rng, dims, cuts, least, largest):
    factor_of = 1.0
    for axis_at, blocks in cuts:
        steps = jax.random.uniform(jax.random.fold_in(jax.random.fold_in(rng, 6), axis_at), (blocks,), jnp.float32, least / len(cuts), largest / len(cuts))
        factor_of = factor_of * jnp.repeat(jnp.exp(steps), dims[axis_at] // blocks).reshape((-1,) + (1,) * (len(dims) - 1 - axis_at))
    return factor_of


def gaussian(stream_key, dims, scale, bound, split=(), kind=jnp.bfloat16):
    entries = scale * jax.random.normal(stream_key, dims, jnp.float32)
    if split:
        entries = entries * steps_of(stream_key, dims, split, -0.22, 0.18)
    return jnp.clip(entries, -bound, bound).astype(kind)


def setup_inputs(seed: int = 0) -> dict:
    seeds = jax.random.split(jax.random.key(seed), 6)
    queries = draw_queries(jax.random.fold_in(seeds[5], 71), 0)
    keys = draw_keys(jax.random.fold_in(seeds[5], 71), 0)
    values = gaussian(seeds[2], (TOKENS, HEADS * HEAD_DIM), 2.0, 12.0, ((0, 128),))
    grad_out = gaussian(seeds[3], (TOKENS, HEADS * HEAD_DIM), 1.0, 6.0, ((0, 128),))
    pattern = draw_pattern(jax.random.fold_in(seeds[5], 71), 0)
    return dict(queries=queries, keys=keys, values=values, grad_out=grad_out, pattern=pattern)


def split_heads(array):
    return array.reshape(NBLOCKS, BLOCK, HEADS, HEAD_DIM).transpose(2, 0, 1, 3)

def merge_heads(array):
    return array.transpose(1, 2, 0, 3).reshape(TOKENS, HEADS * HEAD_DIM)

def reference(queries, keys, values, grad_out, pattern):
    score_scale = 1.0 / math.sqrt(HEAD_DIM)
    causal = jnp.arange(BLOCK)[:, None] >= jnp.arange(BLOCK)[None, :]

    def one_head(operands):
        query_blocks, key_blocks, value_blocks, grad_blocks = operands

        def attend(totals, block_index):
            key_grads, value_grads = totals
            pattern_row = pattern[block_index]
            valid = pattern_row >= 0
            safe_rows = jnp.maximum(pattern_row, 0).astype(jnp.int32)
            chosen_keys = key_blocks[safe_rows].reshape(SLOTS * BLOCK, HEAD_DIM)
            chosen_values = value_blocks[safe_rows].reshape(SLOTS * BLOCK, HEAD_DIM)
            query_block = query_blocks[block_index]
            grad_block = grad_blocks[block_index]
            scores = jnp.dot(query_block, chosen_keys.T, preferred_element_type=jnp.float32) * score_scale
            earlier = (pattern_row < block_index)[:, None, None] | causal[None]
            allowed = valid[:, None, None] & earlier
            allowed = allowed.transpose(1, 0, 2).reshape(BLOCK, SLOTS * BLOCK)
            masked = jnp.where(allowed, scores, -jnp.inf)
            row_top = lax.optimization_barrier(jnp.max(masked, axis=1, keepdims=True))
            exponent = jnp.where(allowed, jnp.exp(masked - row_top), 0.0)
            weights_wide = exponent / lax.optimization_barrier(jnp.sum(exponent, axis=1, keepdims=True))
            weights = weights_wide.astype(jnp.bfloat16)
            output_wide = jnp.dot(weights, chosen_values, preferred_element_type=jnp.float32)
            grad_weights = jnp.dot(grad_block, chosen_values.T, preferred_element_type=jnp.float32)
            row_delta = lax.optimization_barrier(jnp.sum(grad_block.astype(jnp.float32) * output_wide, axis=1, keepdims=True))
            grad_scores = (score_scale * weights_wide * (grad_weights - row_delta)).astype(jnp.bfloat16)
            grad_query = jnp.dot(grad_scores, chosen_keys, preferred_element_type=jnp.float32)
            key_terms = jnp.dot(grad_scores.T, query_block, preferred_element_type=jnp.float32)
            value_terms = jnp.dot(weights.T, grad_block, preferred_element_type=jnp.float32)
            key_grads = key_grads.at[safe_rows].add(key_terms.reshape(SLOTS, BLOCK, HEAD_DIM))
            value_grads = value_grads.at[safe_rows].add(value_terms.reshape(SLOTS, BLOCK, HEAD_DIM))
            return ((key_grads, value_grads), (output_wide.astype(jnp.bfloat16), grad_query.astype(jnp.bfloat16)))
        start = jnp.zeros((NBLOCKS, BLOCK, HEAD_DIM), jnp.float32)
        (key_grads, value_grads), (outputs, query_grads) = lax.scan(attend, (start, start), jnp.arange(NBLOCKS, dtype=jnp.int32))
        return (outputs, query_grads, key_grads.astype(jnp.bfloat16), value_grads.astype(jnp.bfloat16))
    results = lax.map(one_head, (split_heads(queries), split_heads(keys), split_heads(values), split_heads(grad_out)))
    return (merge_heads(results[0]), merge_heads(results[1]), merge_heads(results[2]), merge_heads(results[3]))
```

```python
import functools
import math

import jax
import jax.numpy as jnp
from jax import lax
from jax.experimental import pallas as pl
from jax.experimental.pallas import tpu as pltpu
from jax.sharding import PartitionSpec as P

D = 128
B = 128
NB = 6
NF = 12
EDGE = 384
T = 768
F32 = jnp.float32
BF = jnp.bfloat16
C2 = math.log2(math.e) / math.sqrt(D)


def nt(a, b):
    return lax.dot_general(a, b, (((1,), (1,)), ((), ())), preferred_element_type=F32)


def tn(a, b):
    return lax.dot_general(a, b, (((0,), (0,)), ((), ())), preferred_element_type=F32)


def nn(a, b):
    return jnp.dot(a, b, preferred_element_type=F32)


def near_span(w):
    return max(0, w - 3) * B, (min(NB - 1, w) + 1) * B


def kern(q_ref, g_ref, kw_ref, vw_ref, kp_ref, vp_ref, fb_ref, nb_ref,
         o_ref, dq_ref, dkw_ref, dvw_ref, dkp_ref, dvp_ref,
         sf, sn, ef, en, m_s, l_s, ot_s, dqt_s):
    q = q_ref[...]
    g = g_ref[...]
    qt = q.T
    tri = lax.broadcasted_iota(jnp.int32, (B, B), 0) <= lax.broadcasted_iota(jnp.int32, (B, B), 1)
    m_s[...] = jnp.full((1, T), -jnp.inf, F32)
    for i in range(NF):
        s = nn(kp_ref[i * B:(i + 1) * B, :], qt)
        sf[i] = s
        m_s[...] = jnp.maximum(m_s[...], jnp.max(s, axis=0, keepdims=True) - fb_ref[i:i + 1, :])
    for w in range(NB + 3):
        lo, hi = near_span(w)
        s = nn(kw_ref[w * B:(w + 1) * B, :], qt[:, lo:hi])
        if w >= 3:
            s = jnp.concatenate([jnp.where(tri, s[:, :B], -jnp.inf), s[:, B:]], 1) if hi - lo > B else jnp.where(tri, s, -jnp.inf)
        sn[w, :, :hi - lo] = s
        m_s[:, lo:hi] = jnp.maximum(m_s[:, lo:hi], jnp.max(s, axis=0, keepdims=True) - nb_ref[w:w + 1, lo:hi])
    m = m_s[...]
    l_s[...] = jnp.zeros((1, T), F32)
    ot_s[...] = jnp.zeros((D, T), F32)
    for i in range(NF):
        e = jnp.exp2((sf[i] - (m + fb_ref[i:i + 1, :])) * C2)
        l_s[...] += jnp.sum(e, axis=0, keepdims=True)
        e = e.astype(BF)
        ef[i] = e
        ot_s[...] += tn(vp_ref[i * B:(i + 1) * B, :], e)
    for w in range(NB + 3):
        lo, hi = near_span(w)
        e = jnp.exp2((sn[w, :, :hi - lo] - (m[:, lo:hi] + nb_ref[w:w + 1, lo:hi])) * C2)
        l_s[:, lo:hi] += jnp.sum(e, axis=0, keepdims=True)
        e = e.astype(BF)
        en[w, :, :hi - lo] = e
        ot_s[:, lo:hi] += tn(vw_ref[w * B:(w + 1) * B, :], e)
    inv = 1.0 / l_s[...]
    ot = ot_s[...] * inv
    o_ref[...] = ot.T.astype(BF)
    gt = (g.T.astype(F32) * inv).astype(BF)
    gs = gt.T
    delta = jnp.sum(gt.astype(F32) * ot, axis=0, keepdims=True)
    dqt_s[...] = jnp.zeros((D, T), F32)
    scale = 1.0 / math.sqrt(D)
    for i in range(NF):
        e = ef[i]
        dvp_ref[i * B:(i + 1) * B, :] = nn(e, gs).astype(BF)
        dp = nn(vp_ref[i * B:(i + 1) * B, :], gt)
        ds = (e.astype(F32) * (dp - delta)).astype(BF)
        dkp_ref[i * B:(i + 1) * B, :] = (nn(ds, q) * scale).astype(BF)
        dqt_s[...] += tn(kp_ref[i * B:(i + 1) * B, :], ds)
    for w in range(NB + 3):
        lo, hi = near_span(w)
        e = en[w, :, :hi - lo]
        dvw_ref[w * B:(w + 1) * B, :] = nn(e, gs[lo:hi])
        dp = nn(vw_ref[w * B:(w + 1) * B, :], gt[:, lo:hi])
        ds = (e.astype(F32) * (dp - delta[:, lo:hi])).astype(BF)
        dkw_ref[w * B:(w + 1) * B, :] = nn(ds, q[lo:hi]) * scale
        dqt_s[:, lo:hi] += tn(kw_ref[w * B:(w + 1) * B, :], ds)
    dq_ref[...] = (dqt_s[...].T * scale).astype(BF)


def attend(q, g, kw, vw, kp, vp, fb, nb):
    def col(rows):
        return pl.BlockSpec((rows, D), lambda h: (0, h))
    full = lambda a: pl.BlockSpec(a.shape, lambda h: (0, 0))
    H = q.shape[1] // D
    W = (NB + 3) * B
    return pl.pallas_call(
        kern,
        grid=(H,),
        in_specs=[col(T), col(T), col(W), col(W), col(NF * B), col(NF * B), full(fb), full(nb)],
        out_specs=[col(T), col(T), col(W), col(W), col(NF * B), col(NF * B)],
        out_shape=[jax.ShapeDtypeStruct((T, H * D), BF)] * 2
        + [jax.ShapeDtypeStruct((W, H * D), F32)] * 2
        + [jax.ShapeDtypeStruct((NF * B, H * D), BF)] * 2,
        scratch_shapes=[
            pltpu.VMEM((NF, B, T), F32),
            pltpu.VMEM((NB + 3, B, 512), F32),
            pltpu.VMEM((NF, B, T), BF),
            pltpu.VMEM((NB + 3, B, 512), BF),
            pltpu.VMEM((1, T), F32),
            pltpu.VMEM((1, T), F32),
            pltpu.VMEM((D, T), F32),
            pltpu.VMEM((D, T), F32),
        ],
        compiler_params=pltpu.CompilerParams(vmem_limit_bytes=48 * 1024 * 1024),
    )(q, g, kw, vw, kp, vp, fb, nb)


def shifted(value, steps):
    count = lax.axis_size("ctx")
    first, last = (max(0, -steps), min(count, count - steps))
    return lax.ppermute(value, "ctx", [(s, s + steps) for s in range(first, last)])


ROW = 8
ROWS = 4
ROW_GROUPS = [[r * ROW + i for i in range(ROW)] for r in range(ROWS)]
COL_GROUPS = [[r * ROW + i for r in range(ROWS)] for i in range(ROW)]


def biases(pattern, phase, device):
    rows = lax.dynamic_slice_in_dim(pattern, device * NB, NB, 0)
    ids = phase + 16 * jnp.arange(NF, dtype=jnp.int32)
    far = jnp.any(rows[None, :, 4:] == ids[:, None, None], axis=2)
    fb = jnp.where(far, 0.0, jnp.inf).astype(F32)
    blocks = device * NB - 3 + jnp.arange(NB + 3, dtype=jnp.int32)
    nb = jnp.where(blocks >= 0, 0.0, jnp.inf).astype(F32)
    return jnp.repeat(fb, B, axis=1), jnp.broadcast_to(nb[:, None], (NB + 3, T))


def per_device(queries, keys, values, grad_out, pattern):
    a2a = functools.partial(lax.all_to_all, axis_name="head", split_axis=1, concat_axis=0, tiled=True)
    k, v, q, g = a2a(keys), a2a(values), a2a(queries), a2a(grad_out)
    device = lax.axis_index("ctx")
    phase = pattern[pattern.shape[0] - 1, 4] % 16
    own = jnp.mod(phase - device * NB, 16)
    valid = own < NB
    own = jnp.where(valid, own, 0) * B
    slot = jnp.where(
        valid,
        jnp.concatenate([lax.dynamic_slice_in_dim(k, own, B, 0), lax.dynamic_slice_in_dim(v, own, B, 0)], 0),
        0,
    )
    row = lax.all_gather(slot, "ctx", axis=0, tiled=True, axis_index_groups=ROW_GROUPS)
    places = [(phase + 16 * j) // NB * (2 * B) for j in range(3)]
    three = jnp.concatenate([lax.dynamic_slice_in_dim(row, p, 2 * B, 0) for p in places], 0)
    pool = lax.all_gather(three, "ctx", axis=0, tiled=True, axis_index_groups=COL_GROUPS)
    pool = pool.reshape(NF, 2, B, 512)
    kp, vp = pool[:, 0].reshape(NF * B, 512), pool[:, 1].reshape(NF * B, 512)
    before_k, before_v = shifted((k[T - EDGE:], v[T - EDGE:]), 1)
    kw, vw = jnp.concatenate([before_k, k], 0), jnp.concatenate([before_v, v], 0)
    fb, nb = biases(pattern, phase, device)
    o, dq, dkw, dvw, dkp, dvp = attend(q, g, kw, vw, kp, vp, fb, nb)
    back_k, back_v = shifted((dkw[:EDGE].astype(BF), dvw[:EDGE].astype(BF)), -1)
    both = jnp.stack([dkp.reshape(NF, B, 512), dvp.reshape(NF, B, 512)], 1).reshape(NF * 2 * B, 512)
    mine3 = lax.psum_scatter(both, "ctx", scatter_dimension=0, tiled=True, axis_index_groups=COL_GROUPS)
    slots = jnp.zeros((ROW * 2 * B, 512), BF)
    for j in range(3):
        slots = lax.dynamic_update_slice_in_dim(slots, mine3[j * 2 * B:(j + 1) * 2 * B], places[j], 0)
    mine = lax.psum_scatter(slots, "ctx", scatter_dimension=0, tiled=True, axis_index_groups=ROW_GROUPS)
    mine = jnp.where(valid, mine.astype(F32), 0.0)

    def merged(ext, back, extra):
        total = ext[EDGE:] + jnp.pad(back.astype(F32), ((T - EDGE, 0), (0, 0)))
        total = lax.dynamic_update_slice_in_dim(
            total, lax.dynamic_slice_in_dim(total, own, B, 0) + extra, own, 0
        )
        return total.astype(BF)

    dk = merged(dkw, back_k, mine[:B])
    dv = merged(dvw, back_v, mine[B:])
    out = functools.partial(lax.all_to_all, axis_name="head", split_axis=0, concat_axis=1, tiled=True)
    return out(o), out(dq), out(dk), out(dv)


def solution(mesh):
    split = P(("ctx", "head"), None)
    return jax.shard_map(
        per_device, mesh=mesh, in_specs=(split,) * 4 + (P(),), out_specs=(split,) * 4, check_vma=False
    )
```

```python
import functools
import math

import jax
import jax.numpy as jnp
from jax import lax
from jax.experimental import pallas as pl
from jax.experimental.pallas import tpu as pltpu
from jax.sharding import PartitionSpec as P

D = 128
B = 128
NB = 6
NF = 12
NW = 9
EDGE = 384
T = 768
W = 1152
R = 192
H = 4
Z = 4
F32 = jnp.float32
BF = jnp.bfloat16
SCALE = 1.0 / math.sqrt(D)
C2 = math.log2(math.e) / math.sqrt(D)
MESH = pl.DeviceIdType.MESH


def tn(a, b):
    return lax.dot_general(a, b, (((0,), (0,)), ((), ())), preferred_element_type=F32)


def nn(a, b):
    return jnp.dot(a, b, preferred_element_type=F32)


def near_span(w):
    return max(0, w - 3) * B, (min(NB - 1, w) + 1) * B


def kernel(
    k_in, v_in, q_in, g_in, pat,
    o_out, dq_out, dk_out, dv_out,
    kb, vb, qb, gb, slot, rows, pool,
    ob, dqb, dkw, dvw, dkb, dvb, back_s, back_r,
    dpool, sib_r, pair, x_r, ysl, y_r, zs, z_r, zown,
    fb, sf, sn, ef, en, m_s, l_s, ot_s, dqt_s, gt_s, gs_s, de_s, qt_s,
    a_s, a_r, h_s, h_r, s1_s, s1_r, y1_s, y1_r, x1_s, x1_r, s2_s, s2_r,
    o_s, o_r, gs_sd, gs_rc, gx_s, gx_rc, gy_s, gy_rc, gz_s, gz_rc, b_s, b_r,
):
    ctx = lax.axis_index("ctx")
    z = lax.axis_index("head")
    c = ctx % 2
    y = (ctx // 2) % 4
    x = ctx // 8
    sib = ctx + 1 - 2 * c
    up = (ctx + 1) % 32
    down = (ctx + 31) % 32

    def xpeer(d):
        return ((x + d) % 4) * 8 + y * 2 + c

    def ypeer(d):
        return x * 8 + ((y + d) % 4) * 2 + c

    def at(ctx_, z_):
        return {"ctx": ctx_, "head": z_}

    def remote(src, dst, ss, rs, dev):
        return pltpu.make_async_remote_copy(
            src_ref=src, dst_ref=dst, send_sem=ss, recv_sem=rs, device_id=dev, device_id_type=MESH
        )

    def done(ref, sem):
        pltpu.make_async_copy(ref, ref, sem).wait()

    barrier = pltpu.get_barrier_semaphore()
    peers = [at(ctx, (z + d) % Z) for d in (1, 2, 3)]
    peers += [at(ypeer(d), z) for d in (1, 2, 3)] + [at(xpeer(d), z) for d in (1, 2, 3)]
    peers += [at(sib, z), at(up, z), at(down, z)]
    for dev in peers:
        pl.semaphore_signal(barrier, inc=1, device_id=dev, device_id_type=MESH)

    phase = pat[NB * 32 - 1, 4] % 16
    own = (phase - ctx * NB + 192) % 16
    ids = phase + 16 * lax.broadcasted_iota(jnp.int32, (16, B), 0)
    for b in range(NB):
        hit = jnp.full((16, B), jnp.inf, F32)
        for s in range(NF):
            hit = jnp.where(ids == pat[ctx * NB + b, 4 + s], 0.0, hit)
        fb[:, b * B:(b + 1) * B] = hit

    @pl.when(ctx == 0)
    def _():
        kb[:, :EDGE, :] = jnp.zeros((H, EDGE, D), BF)
        vb[:, :EDGE, :] = jnp.zeros((H, EDGE, D), BF)

    @pl.when(ctx == 31)
    def _():
        back_r[...] = jnp.zeros((2, H, EDGE, D), BF)

    pl.semaphore_wait(barrier, len(peers))

    arrays = ((k_in, kb, EDGE), (v_in, vb, EDGE), (q_in, qb, 0), (g_in, gb, 0))

    def lanes(group, h):
        return pl.ds(pl.multiple_of((group * H + h) * D, D), D)

    def a_start(h):
        for n, (src, dst, base) in enumerate(arrays):
            place = dst.at[h, pl.ds(pl.multiple_of(base + z * R, 64), R), :]
            for d in (2, 1, 3):
                to = (z + d) % Z
                remote(src.at[:, lanes(to, h)], place, a_s.at[n, h], a_r.at[n, h], at(ctx, to)).start()
            pltpu.make_async_copy(src.at[:, lanes(z, h)], place, a_r.at[n, h]).start()

    def b_stage(h):
        done(kb.at[h, EDGE:, :], a_r.at[0, h])
        done(vb.at[h, EDGE:, :], a_r.at[1, h])

        @pl.when(ctx < 31)
        def _():
            remote(kb.at[h, W - EDGE:, :], kb.at[h, :EDGE, :], h_s.at[0, h], h_r.at[0, h], at(up, z)).start()
            remote(vb.at[h, W - EDGE:, :], vb.at[h, :EDGE, :], h_s.at[1, h], h_r.at[1, h], at(up, z)).start()

        ks = jnp.zeros((B, D), BF)
        vs = jnp.zeros((B, D), BF)
        for b in range(NB):
            r = slice(EDGE + b * B, EDGE + (b + 1) * B)
            ks = jnp.where(own == b, kb[h, r, :], ks)
            vs = jnp.where(own == b, vb[h, r, :], vs)
        rows[h, y, c] = jnp.where(c == 0, ks, vs)
        slot[h] = jnp.where(c == 0, vs, ks)
        remote(slot.at[h], rows.at[h, y, c], s1_s.at[h], s1_r.at[h], at(sib, z)).start()

    def c_stage(h):
        done(slot.at[h], s1_r.at[h])
        for d in (2, 1, 3):
            remote(rows.at[h, y], rows.at[h, y], y1_s.at[h], y1_r.at[h], at(ypeer(d), z)).start()

    def d_stage(h):
        done(rows.at[h, :3], y1_r.at[h])
        for j in range(3):
            place = (phase + 16 * j) // NB
            blk = jnp.zeros((B, D), BF)
            for s in range(3 * j if j < 2 else 5, (3, 6, 8)[j]):
                blk = jnp.where(place == s, rows[h, s // 2, s % 2], blk)
            if j == 1:
                blk = jnp.where(place == 2, rows[h, 1, 0], blk)
            pool[h, c, 3 * x + j] = blk
        mine = pool.at[h, c, pl.ds(3 * x, 3)]
        for d in (2, 1, 3):
            remote(mine, mine, x1_s.at[h], x1_r.at[h], at(xpeer(d), z)).start()

    def e_stage(h):
        done(pool.at[h, c, :9], x1_r.at[h])
        remote(pool.at[h, c], pool.at[h, c], s2_s.at[h], s2_r.at[h], at(sib, z)).start()

    def f_stage(h):
        done(qb.at[h], a_r.at[2, h])
        done(gb.at[h], a_r.at[3, h])

        @pl.when(ctx > 0)
        def _():
            done(kb.at[h, :EDGE, :], h_r.at[0, h])
            done(vb.at[h, :EDGE, :], h_r.at[1, h])

        done(pool.at[h, 0], s2_r.at[h])

    tri = lax.broadcasted_iota(jnp.int32, (B, B), 0) <= lax.broadcasted_iota(jnp.int32, (B, B), 1)

    def near_off(w):
        return jnp.where(ctx * NB - 3 + w >= 0, 0.0, jnp.inf).astype(F32)

    def pass1(h):
        qt_s[...] = qb[h].T
        m_s[...] = jnp.full((1, T), -jnp.inf, F32)
        for i in range(NF):
            s = nn(pool[h, 0, i], qt_s[...])
            sf[i] = s
            m_s[...] = jnp.maximum(m_s[...], jnp.max(s, axis=0, keepdims=True) - fb[i:i + 1, :])
        for w in range(NW):
            lo, hi = near_span(w)
            s = nn(kb[h, w * B:(w + 1) * B, :], qt_s[:, lo:hi])
            if w >= 3:
                first = jnp.where(tri, s[:, :B], -jnp.inf)
                s = jnp.concatenate([first, s[:, B:]], 1) if hi - lo > B else first
            sn[w, :, :hi - lo] = s
            top = jnp.max(s, axis=0, keepdims=True)
            if w < 3:
                top = top - near_off(w)
            m_s[:, lo:hi] = jnp.maximum(m_s[:, lo:hi], top)

    def pass2(h):
        m = m_s[...]
        l_s[...] = jnp.zeros((1, T), F32)
        ot_s[...] = jnp.zeros((D, T), F32)
        for i in range(NF):
            e = jnp.exp2((sf[i] - (m + fb[i:i + 1, :])) * C2)
            l_s[...] += jnp.sum(e, axis=0, keepdims=True)
            e = e.astype(BF)
            ef[i] = e
            ot_s[...] += tn(pool[h, 1, i], e)
        for w in range(NW):
            lo, hi = near_span(w)
            ref = m[:, lo:hi]
            if w < 3:
                ref = ref + near_off(w)
            e = jnp.exp2((sn[w, :, :hi - lo] - ref) * C2)
            l_s[:, lo:hi] += jnp.sum(e, axis=0, keepdims=True)
            e = e.astype(BF)
            en[w, :, :hi - lo] = e
            ot_s[:, lo:hi] += tn(vb[h, w * B:(w + 1) * B, :], e)
        inv = 1.0 / l_s[...]
        ot = ot_s[...] * inv
        ob[h] = ot.T.astype(BF)
        gt = (gb[h].T.astype(F32) * inv).astype(BF)
        gt_s[...] = gt
        gs_s[...] = gt.T
        de_s[...] = jnp.sum(gt.astype(F32) * ot, axis=0, keepdims=True)

    def pass3(h):
        dqt_s[...] = jnp.zeros((D, T), F32)
        for i in range(NF):
            e = ef[i]
            dpool[h, 1, i] = nn(e, gs_s[...]).astype(BF)
            dp = nn(pool[h, 1, i], gt_s[...])
            ds = (e.astype(F32) * (dp - de_s[...])).astype(BF)
            dpool[h, 0, i] = (nn(ds, qb[h]) * SCALE).astype(BF)
            dqt_s[...] += tn(pool[h, 0, i], ds)
        for w in range(NW):
            lo, hi = near_span(w)
            r = slice(w * B, (w + 1) * B)
            e = en[w, :, :hi - lo]
            dv = nn(e, gs_s[lo:hi, :])
            dp = nn(vb[h, r, :], gt_s[:, lo:hi])
            ds = (e.astype(F32) * (dp - de_s[:, lo:hi])).astype(BF)
            dk = nn(ds, qb[h, lo:hi, :]) * SCALE
            if w < 3:
                back_s[0, h, r, :] = dk.astype(BF)
                back_s[1, h, r, :] = dv.astype(BF)
            else:
                r = slice((w - 3) * B, (w - 2) * B)
                dkw[h, r, :] = dk
                dvw[h, r, :] = dv
            dqt_s[:, lo:hi] += tn(kb[h, w * B:(w + 1) * B, :], ds)
        dqb[h] = (dqt_s[...].T * SCALE).astype(BF)

    outs = ((ob, o_out), (dqb, dq_out), (dkb, dk_out), (dvb, dv_out))

    def o_start(n, h):
        src, dst = outs[n]
        place = dst.at[:, lanes(z, h)]
        for d in (2, 1, 3):
            to = (z + d) % Z
            part = src.at[h, pl.ds(pl.multiple_of(to * R, 64), R), :]
            remote(part, place, o_s.at[n, h], o_r.at[n, h], at(ctx, to)).start()
        part = src.at[h, pl.ds(pl.multiple_of(z * R, 64), R), :]
        pltpu.make_async_copy(part, place, o_r.at[n, h]).start()

    def g0(h):
        remote(dpool.at[h, 1 - c], sib_r.at[h], gs_sd.at[h], gs_rc.at[h], at(sib, z)).start()

        @pl.when(ctx > 0)
        def _():
            for n in range(2):
                remote(back_s.at[n, h], back_r.at[n, h], b_s.at[n, h], b_r.at[n, h], at(down, z)).start()

        o_start(1, h)

    def g1(h):
        done(sib_r.at[h], gs_rc.at[h])
        for i in range(NF):
            pair[h, i] = (dpool[h, c, i].astype(F32) + sib_r[h, i].astype(F32)).astype(BF)
        for d in (2, 1, 3):
            to = (x + d) % 4
            remote(pair.at[h, pl.ds(3 * to, 3)], x_r.at[h, d - 1], gx_s.at[h], gx_rc.at[h], at(xpeer(d), z)).start()

    def g2(h):
        done(x_r.at[h], gx_rc.at[h])
        tot = []
        for j in range(3):
            t = pair[h, 3 * x + j].astype(F32)
            for d in range(3):
                t = t + x_r[h, d, j].astype(F32)
            tot.append(t)
        for s in range(8):
            t = jnp.zeros((B, D), F32)
            for j in range(3):
                if 16 * j <= s * NB + 5 and s * NB <= 16 * j + 15:
                    t = jnp.where((phase + 16 * j) // NB == s, tot[j], t)
            ysl[h, s // 2, s % 2] = t.astype(BF)
        for d in (2, 1, 3):
            to = (y + d) % 4
            remote(ysl.at[h, to], y_r.at[h, d - 1], gy_s.at[h], gy_rc.at[h], at(ypeer(d), z)).start()

    def g3(h):
        done(y_r.at[h], gy_rc.at[h])
        for dst, core in ((zown, c), (zs, 1 - c)):
            t = ysl[h, y, core].astype(F32)
            for d in range(3):
                t = t + y_r[h, d, core].astype(F32)
            dst[h] = t.astype(BF)
        remote(zs.at[h], z_r.at[h], gz_s.at[h], gz_rc.at[h], at(sib, z)).start()

    def g4(h):
        done(z_r.at[h], gz_rc.at[h])

        @pl.when(ctx < 31)
        def _():
            done(back_r.at[0, h], b_r.at[0, h])
            done(back_r.at[1, h], b_r.at[1, h])

        mine, other = zown[h].astype(F32), z_r[h].astype(F32)
        for n, (part, total, dst) in enumerate(
            ((jnp.where(c == 0, mine, other), dkw, dkb), (jnp.where(c == 0, other, mine), dvw, dvb))
        ):
            for b in range(NB):
                r = slice(b * B, (b + 1) * B)
                t = total[h, r, :] + jnp.where(own == b, part, 0.0)
                if b >= 3:
                    t = t + back_r[n, h, (b - 3) * B:(b - 2) * B, :].astype(F32)
                dst[h, r, :] = t.astype(BF)
        o_start(2, h)
        o_start(3, h)

    a_start(0)
    a_start(1)
    b_stage(0)
    c_stage(0)
    d_stage(0)
    e_stage(0)

    @pl.loop(0, H)
    def _(t):
        ahead = t + 1 < H
        after = t > 0

        @pl.when(t + 2 < H)
        def _():
            a_start(t + 2)

        @pl.when(ahead)
        def _():
            b_stage(t + 1)

        @pl.when(after)
        def _():
            g1(t - 1)

        f_stage(t)
        pass1(t)

        @pl.when(ahead)
        def _():
            c_stage(t + 1)

        @pl.when(after)
        def _():
            g2(t - 1)

        pass2(t)
        o_start(0, t)

        @pl.when(ahead)
        def _():
            d_stage(t + 1)

        @pl.when(after)
        def _():
            g3(t - 1)

        pass3(t)
        g0(t)

        @pl.when(ahead)
        def _():
            e_stage(t + 1)

        @pl.when(after)
        def _():
            g4(t - 1)

    g1(H - 1)
    g2(H - 1)
    g3(H - 1)
    g4(H - 1)

    @pl.loop(0, H)
    def _(h):
        for n in range(4):
            done(qb.at[h, :3 * R, :], a_s.at[n, h])
            done(qb.at[h, :3 * R, :], o_s.at[n, h])
            done(qb.at[h], o_r.at[n, h])
        done(slot.at[h], s1_s.at[h])
        done(rows.at[h, :3], y1_s.at[h])
        done(pool.at[h, 0, :9], x1_s.at[h])
        done(pool.at[h, 0], s2_s.at[h])
        done(sib_r.at[h], gs_sd.at[h])
        done(x_r.at[h], gx_s.at[h])
        done(y_r.at[h], gy_s.at[h])
        done(z_r.at[h], gz_s.at[h])

        @pl.when(ctx < 31)
        def _():
            done(back_r.at[0, h], h_s.at[0, h])
            done(back_r.at[0, h], h_s.at[1, h])

        @pl.when(ctx > 0)
        def _():
            done(back_r.at[0, h], b_s.at[0, h])
            done(back_r.at[0, h], b_s.at[1, h])


def per_device(queries, keys, values, grad_out, pattern):
    vm = pltpu.VMEM
    dma = pltpu.SemaphoreType.DMA
    return pl.pallas_call(
        kernel,
        out_shape=[jax.ShapeDtypeStruct((R, H * Z * D), BF)] * 4,
        in_specs=[pl.BlockSpec(memory_space=pl.ANY)] * 4 + [pl.BlockSpec(memory_space=pltpu.SMEM)],
        out_specs=[pl.BlockSpec(memory_space=pl.ANY)] * 4,
        scratch_shapes=[
            vm((H, W, D), BF), vm((H, W, D), BF), vm((H, T, D), BF), vm((H, T, D), BF),
            vm((H, B, D), BF), vm((H, 4, 2, B, D), BF), vm((H, 2, NF, B, D), BF),
            vm((H, T, D), BF), vm((H, T, D), BF), vm((H, T, D), F32), vm((H, T, D), F32),
            vm((H, T, D), BF), vm((H, T, D), BF), vm((2, H, EDGE, D), BF), vm((2, H, EDGE, D), BF),
            vm((H, 2, NF, B, D), BF), vm((H, NF, B, D), BF), vm((H, NF, B, D), BF),
            vm((H, 3, 3, B, D), BF), vm((H, 4, 2, B, D), BF), vm((H, 3, 2, B, D), BF),
            vm((H, B, D), BF), vm((H, B, D), BF), vm((H, B, D), BF),
            vm((16, T), F32), vm((NF, B, T), F32), vm((NW, B, 512), F32), vm((NF, B, T), BF), vm((NW, B, 512), BF),
            vm((1, T), F32), vm((1, T), F32), vm((D, T), F32), vm((D, T), F32),
            vm((D, T), BF), vm((T, D), BF), vm((1, T), F32), vm((D, T), BF),
            dma((4, H)), dma((4, H)), dma((2, H)), dma((2, H)), dma((H,)), dma((H,)), dma((H,)), dma((H,)),
            dma((H,)), dma((H,)), dma((H,)), dma((H,)),
            dma((4, H)), dma((4, H)), dma((H,)), dma((H,)), dma((H,)), dma((H,)), dma((H,)), dma((H,)),
            dma((H,)), dma((H,)), dma((2, H)), dma((2, H)),
        ],
        compiler_params=pltpu.CompilerParams(
            collective_id=0, has_side_effects=True, vmem_limit_bytes=58 * 1024 * 1024
        ),
    )(keys, values, queries, grad_out, pattern)


def solution(mesh):
    split = P(("ctx", "head"), None)
    return jax.shard_map(
        per_device, mesh=mesh, in_specs=(split,) * 4 + (P(),), out_specs=(split,) * 4, check_vma=False
    )
```

```python
import functools
import math

import jax
import jax.numpy as jnp
from jax import lax
from jax.experimental import pallas as pl
from jax.experimental.pallas import tpu as pltpu
from jax.sharding import PartitionSpec as P

D = 128
B = 128
NB = 6
NF = 12
NW = 9
EDGE = 384
T = 768
W = 1152
R = 192
H = 4
Z = 4
F32 = jnp.float32
BF = jnp.bfloat16
SCALE = 1.0 / math.sqrt(D)
C2 = math.log2(math.e) / math.sqrt(D)
MESH = pl.DeviceIdType.MESH
KV = (0, 1)
QG = (2, 3)


def tn(a, b):
    return lax.dot_general(a, b, (((0,), (0,)), ((), ())), preferred_element_type=F32)


def nn(a, b):
    return jnp.dot(a, b, preferred_element_type=F32)


def near_span(w):
    return max(0, w - 3) * B, (min(NB - 1, w) + 1) * B


def kernel(
    k_in, v_in, q_in, g_in, pat,
    o_out, dq_out, dk_out, dv_out,
    kb, vb, qb, gb, slot, rows, pool,
    ob, dqb, dkw, dvw, dkb, dvb, back_s, back_r,
    dpool, sib_r, pair, x_r, ysl, y_r,
    fb, sf, sn, ef, en, m_s, l_s, ot_s, dqt_s, gt_s, gs_s, de_s, qt_s,
    a_s, a_r, h_s, h_r, y1_s, y1_r, x1_s, x1_r, s2_s, s2_r,
    o_s, o_r, gs_sd, gs_rc, gx_s, gx_rc, gy_s, gy_rc, b_s, b_r,
):
    ctx = lax.axis_index("ctx")
    z = lax.axis_index("head")
    c = ctx % 2
    y = (ctx // 2) % 4
    x = ctx // 8
    sib = ctx + 1 - 2 * c
    up = (ctx + 1) % 32
    down = (ctx + 31) % 32

    def xpeer(d):
        return ((x + d) % 4) * 8 + y * 2 + c

    def rowpeer(d, other):
        return ((y + d) % 4) * 2 + (1 - c if other else c)

    row_moves = [(d, other) for other in (0, 1) for d in (2, 1, 3)] + [(0, 1)]
    me8 = y * 2 + c

    def at(ctx_, z_):
        return {"ctx": ctx_, "head": z_}

    def remote(src, dst, ss, rs, dev):
        return pltpu.make_async_remote_copy(
            src_ref=src, dst_ref=dst, send_sem=ss, recv_sem=rs, device_id=dev, device_id_type=MESH
        )

    def done(ref, sem):
        pltpu.make_async_copy(ref, ref, sem).wait()

    barrier = pltpu.get_barrier_semaphore()
    peers = [at(ctx, (z + d) % Z) for d in (1, 2, 3)]
    peers += [at(x * 8 + rowpeer(*m), z) for m in row_moves] + [at(xpeer(d), z) for d in (1, 2, 3)]
    peers += [at(up, z), at(down, z)]
    for dev in peers:
        pl.semaphore_signal(barrier, inc=1, device_id=dev, device_id_type=MESH)

    phase = pat[4, NB * 32 - 1] % 16
    own = (phase - ctx * NB + 192) % 16
    ids = phase + 16 * lax.broadcasted_iota(jnp.int32, (16, B), 0)
    for b in range(NB):
        hit = jnp.full((16, B), jnp.inf, F32)
        for s in range(NF):
            hit = jnp.where(ids == pat[4 + s, ctx * NB + b], 0.0, hit)
        fb[:, b * B:(b + 1) * B] = hit

    @pl.when(ctx == 0)
    def _():
        kb[:, :EDGE, :] = jnp.zeros((H, EDGE, D), BF)
        vb[:, :EDGE, :] = jnp.zeros((H, EDGE, D), BF)

    @pl.when(ctx == 31)
    def _():
        back_r[...] = jnp.zeros((2, H, EDGE, D), BF)

    pl.semaphore_wait(barrier, len(peers))

    arrays = ((k_in, kb, EDGE), (v_in, vb, EDGE), (q_in, qb, 0), (g_in, gb, 0))

    def lanes(group, h):
        return pl.ds(pl.multiple_of((group * H + h) * D, D), D)

    def a_start(h, which):
        for n in which:
            src, dst, base = arrays[n]
            place = dst.at[h, pl.ds(pl.multiple_of(base + z * R, 64), R), :]
            for d in (2, 1, 3):
                to = (z + d) % Z
                remote(src.at[:, lanes(to, h)], place, a_s.at[n, h], a_r.at[n, h], at(ctx, to)).start()
            pltpu.make_async_copy(src.at[:, lanes(z, h)], place, a_r.at[n, h]).start()

    def b_stage(h):
        done(kb.at[h, EDGE:, :], a_r.at[0, h])
        done(vb.at[h, EDGE:, :], a_r.at[1, h])

        @pl.when(ctx < 31)
        def _():
            remote(kb.at[h, W - EDGE:, :], kb.at[h, :EDGE, :], h_s.at[0, h], h_r.at[0, h], at(up, z)).start()
            remote(vb.at[h, W - EDGE:, :], vb.at[h, :EDGE, :], h_s.at[1, h], h_r.at[1, h], at(up, z)).start()

        ks = jnp.zeros((B, D), BF)
        vs = jnp.zeros((B, D), BF)
        for b in range(NB):
            r = slice(EDGE + b * B, EDGE + (b + 1) * B)
            ks = jnp.where(own == b, kb[h, r, :], ks)
            vs = jnp.where(own == b, vb[h, r, :], vs)
        rows[h, me8] = jnp.where(c == 0, ks, vs)
        slot[h] = jnp.where(c == 0, vs, ks)
        for d, other in row_moves:
            src = slot.at[h] if other else rows.at[h, me8]
            to = at(x * 8 + rowpeer(d, other), z)
            remote(src, rows.at[h, me8], y1_s.at[h], y1_r.at[h], to).start()

    def d_stage(h):
        done(rows.at[h, :7], y1_r.at[h])
        for j in range(3):
            place = (phase + 16 * j) // NB
            blk = jnp.zeros((B, D), BF)
            for s in range(3 * j if j < 2 else 5, (3, 6, 8)[j]):
                blk = jnp.where(place == s, rows[h, s], blk)
            if j == 1:
                blk = jnp.where(place == 2, rows[h, 2], blk)
            pool[h, c, 3 * x + j] = blk
        mine = pool.at[h, c, pl.ds(3 * x, 3)]
        for d in (2, 1, 3):
            remote(mine, mine, x1_s.at[h], x1_r.at[h], at(xpeer(d), z)).start()

    def e_stage(h):
        done(pool.at[h, c, :9], x1_r.at[h])
        remote(pool.at[h, c], pool.at[h, c], s2_s.at[h], s2_r.at[h], at(sib, z)).start()

    def f_stage(h):
        done(qb.at[h], a_r.at[2, h])
        done(gb.at[h], a_r.at[3, h])

        @pl.when(ctx > 0)
        def _():
            done(kb.at[h, :EDGE, :], h_r.at[0, h])
            done(vb.at[h, :EDGE, :], h_r.at[1, h])

    def f2_stage(h):
        done(pool.at[h, 0], s2_r.at[h])

    tri = lax.broadcasted_iota(jnp.int32, (B, B), 0) <= lax.broadcasted_iota(jnp.int32, (B, B), 1)

    def near_off(w):
        return jnp.where(ctx * NB - 3 + w >= 0, 0.0, jnp.inf).astype(F32)

    def near1(h):
        qt_s[...] = qb[h].T
        m_s[...] = jnp.full((1, T), -jnp.inf, F32)
        for w in range(NW):
            lo, hi = near_span(w)
            s = nn(kb[h, w * B:(w + 1) * B, :], qt_s[:, lo:hi])
            if w >= 3:
                first = jnp.where(tri, s[:, :B], -jnp.inf)
                s = jnp.concatenate([first, s[:, B:]], 1) if hi - lo > B else first
            sn[w, :, :hi - lo] = s
            top = jnp.max(s, axis=0, keepdims=True)
            if w < 3:
                top = top - near_off(w)
            m_s[:, lo:hi] = jnp.maximum(m_s[:, lo:hi], top)

    def far1(h):
        for i in range(NF):
            s = nn(pool[h, 0, i], qt_s[...])
            sf[i] = s
            m_s[...] = jnp.maximum(m_s[...], jnp.max(s, axis=0, keepdims=True) - fb[i:i + 1, :])

    def pass2(h):
        m = m_s[...]
        l_s[...] = jnp.zeros((1, T), F32)
        ot_s[...] = jnp.zeros((D, T), F32)
        for i in range(NF):
            e = jnp.exp2((sf[i] - (m + fb[i:i + 1, :])) * C2)
            l_s[...] += jnp.sum(e, axis=0, keepdims=True)
            e = e.astype(BF)
            ef[i] = e
            ot_s[...] += tn(pool[h, 1, i], e)
        for w in range(NW):
            lo, hi = near_span(w)
            ref = m[:, lo:hi]
            if w < 3:
                ref = ref + near_off(w)
            e = jnp.exp2((sn[w, :, :hi - lo] - ref) * C2)
            l_s[:, lo:hi] += jnp.sum(e, axis=0, keepdims=True)
            e = e.astype(BF)
            en[w, :, :hi - lo] = e
            ot_s[:, lo:hi] += tn(vb[h, w * B:(w + 1) * B, :], e)
        inv = 1.0 / l_s[...]
        ot = ot_s[...] * inv
        ob[h] = ot.T.astype(BF)
        gt = (gb[h].T.astype(F32) * inv).astype(BF)
        gt_s[...] = gt
        gs_s[...] = gt.T
        de_s[...] = jnp.sum(gt.astype(F32) * ot, axis=0, keepdims=True)

    def far3(h):
        dqt_s[...] = jnp.zeros((D, T), F32)
        for i in range(NF):
            e = ef[i]
            dpool[h, 1, i] = nn(e, gs_s[...]).astype(BF)
            dp = nn(pool[h, 1, i], gt_s[...])
            ds = (e.astype(F32) * (dp - de_s[...])).astype(BF)
            dpool[h, 0, i] = (nn(ds, qb[h]) * SCALE).astype(BF)
            dqt_s[...] += tn(pool[h, 0, i], ds)

    def near3(h):
        for w in range(NW):
            lo, hi = near_span(w)
            r = slice(w * B, (w + 1) * B)
            e = en[w, :, :hi - lo]
            dv = nn(e, gs_s[lo:hi, :])
            dp = nn(vb[h, r, :], gt_s[:, lo:hi])
            ds = (e.astype(F32) * (dp - de_s[:, lo:hi])).astype(BF)
            dk = nn(ds, qb[h, lo:hi, :]) * SCALE
            if w < 3:
                back_s[0, h, r, :] = dk.astype(BF)
                back_s[1, h, r, :] = dv.astype(BF)
            else:
                r = slice((w - 3) * B, (w - 2) * B)
                dkw[h, r, :] = dk
                dvw[h, r, :] = dv
            dqt_s[:, lo:hi] += tn(kb[h, w * B:(w + 1) * B, :], ds)
        dqb[h] = (dqt_s[...].T * SCALE).astype(BF)

    outs = ((ob, o_out), (dqb, dq_out), (dkb, dk_out), (dvb, dv_out))

    def o_start(n, h):
        src, dst = outs[n]
        place = dst.at[:, lanes(z, h)]
        for d in (2, 1, 3):
            to = (z + d) % Z
            part = src.at[h, pl.ds(pl.multiple_of(to * R, 64), R), :]
            remote(part, place, o_s.at[n, h], o_r.at[n, h], at(ctx, to)).start()
        part = src.at[h, pl.ds(pl.multiple_of(z * R, 64), R), :]
        pltpu.make_async_copy(part, place, o_r.at[n, h]).start()

    def sib_send(h):
        remote(dpool.at[h, 1 - c], sib_r.at[h], gs_sd.at[h], gs_rc.at[h], at(sib, z)).start()

    def g0(h):
        @pl.when(ctx > 0)
        def _():
            for n in range(2):
                remote(back_s.at[n, h], back_r.at[n, h], b_s.at[n, h], b_r.at[n, h], at(down, z)).start()

        o_start(1, h)

    def g1(h):
        done(sib_r.at[h], gs_rc.at[h])
        for i in range(NF):
            pair[h, i] = (dpool[h, c, i].astype(F32) + sib_r[h, i].astype(F32)).astype(BF)
        for d in (2, 1, 3):
            to = (x + d) % 4
            remote(pair.at[h, pl.ds(3 * to, 3)], x_r.at[h, d - 1], gx_s.at[h], gx_rc.at[h], at(xpeer(d), z)).start()

    def g2(h):
        done(x_r.at[h], gx_rc.at[h])
        tot = []
        for j in range(3):
            t = pair[h, 3 * x + j].astype(F32)
            for d in range(3):
                t = t + x_r[h, d, j].astype(F32)
            tot.append(t)
        for s in range(8):
            t = jnp.zeros((B, D), F32)
            for j in range(3):
                if 16 * j <= s * NB + 5 and s * NB <= 16 * j + 15:
                    t = jnp.where((phase + 16 * j) // NB == s, tot[j], t)
            ysl[h, s] = t.astype(BF)
        for d, other in row_moves:
            to = rowpeer(d, other)
            remote(ysl.at[h, to], y_r.at[h, me8], gy_s.at[h], gy_rc.at[h], at(x * 8 + to, z)).start()
        y_r[h, me8] = ysl[h, me8]

    def g3(h):
        done(y_r.at[h, :7], gy_rc.at[h])

        @pl.when(ctx < 31)
        def _():
            done(back_r.at[0, h], b_r.at[0, h])
            done(back_r.at[1, h], b_r.at[1, h])

        for n, (part, total, dst) in enumerate(
            ((y_r, dkw, dkb), (y_r, dvw, dvb))
        ):
            part = part[h, n].astype(F32) + part[h, 2 + n].astype(F32) + part[h, 4 + n].astype(F32) + part[h, 6 + n].astype(F32)
            for b in range(NB):
                r = slice(b * B, (b + 1) * B)
                t = total[h, r, :] + jnp.where(own == b, part, 0.0)
                if b >= 3:
                    t = t + back_r[n, h, (b - 3) * B:(b - 2) * B, :].astype(F32)
                dst[h, r, :] = t.astype(BF)
        o_start(2, h)
        o_start(3, h)

    for h, which in ((0, KV), (1, KV), (2, KV), (0, QG), (3, KV), (1, QG), (2, QG), (3, QG)):
        a_start(h, which)
    b_stage(0)
    b_stage(1)
    d_stage(0)
    b_stage(2)
    d_stage(1)
    e_stage(0)
    d_stage(2)

    @pl.loop(0, H)
    def _(t):
        f_stage(t)
        near1(t)

        @pl.when(t >= 1)
        def _():
            g1(t - 1)

        f2_stage(t)
        far1(t)

        @pl.when(t == 0)
        def _():
            b_stage(3)

        @pl.when(t + 1 < H)
        def _():
            e_stage(t + 1)

        @pl.when(t >= 2)
        def _():
            g3(t - 2)

        pass2(t)
        o_start(0, t)
        far3(t)
        sib_send(t)

        @pl.when(t == 0)
        def _():
            d_stage(3)

        @pl.when(t >= 1)
        def _():
            g2(t - 1)

        near3(t)
        g0(t)

    g1(H - 1)
    g3(H - 2)
    g2(H - 1)
    g3(H - 1)

    @pl.loop(0, H)
    def _(h):
        for n in range(4):
            done(qb.at[h, :3 * R, :], a_s.at[n, h])
            done(qb.at[h, :3 * R, :], o_s.at[n, h])
            done(qb.at[h], o_r.at[n, h])
        done(rows.at[h, :7], y1_s.at[h])
        done(pool.at[h, 0, :9], x1_s.at[h])
        done(pool.at[h, 0], s2_s.at[h])
        done(sib_r.at[h], gs_sd.at[h])
        done(x_r.at[h], gx_s.at[h])
        done(y_r.at[h, :7], gy_s.at[h])

        @pl.when(ctx < 31)
        def _():
            done(back_r.at[0, h], h_s.at[0, h])
            done(back_r.at[0, h], h_s.at[1, h])

        @pl.when(ctx > 0)
        def _():
            done(back_r.at[0, h], b_s.at[0, h])
            done(back_r.at[0, h], b_s.at[1, h])


def settle(*refs):
    src, dst, held, in_sem, out_sem = refs[:4], refs[4:8], refs[8], refs[9], refs[10]
    half = R // 2
    parts = [(n, slice(m * half, (m + 1) * half), 2 * n + m) for n in range(4) for m in range(2)]
    ins = [pltpu.make_async_copy(src[n].at[r], held.at[n, r], in_sem.at[i]) for n, r, i in parts]
    outs = [pltpu.make_async_copy(held.at[n, r], dst[n].at[r], out_sem.at[i]) for n, r, i in parts]
    for copy in ins:
        copy.start()
    for first, second in zip(ins, outs):
        first.wait()
        second.start()
    for copy in outs:
        copy.wait()


def finish(results):
    return pl.pallas_call(
        settle,
        out_shape=[jax.ShapeDtypeStruct((R, H * Z * D), BF)] * 4,
        in_specs=[pl.BlockSpec(memory_space=pl.ANY)] * 4,
        out_specs=[pl.BlockSpec(memory_space=pl.ANY)] * 4,
        scratch_shapes=[
            pltpu.VMEM((4, R, H * Z * D), BF),
            pltpu.SemaphoreType.DMA((8,)),
            pltpu.SemaphoreType.DMA((8,)),
        ],
        compiler_params=pltpu.CompilerParams(vmem_limit_bytes=58 * 1024 * 1024),
    )(*results)


def per_device(queries, keys, values, grad_out, pattern):
    vm = pltpu.VMEM
    dma = pltpu.SemaphoreType.DMA
    results = pl.pallas_call(
        kernel,
        out_shape=[jax.ShapeDtypeStruct((R, H * Z * D), BF)] * 4,
        in_specs=[pl.BlockSpec(memory_space=pl.ANY)] * 4 + [pl.BlockSpec(memory_space=pltpu.SMEM)],
        out_specs=[pl.BlockSpec(memory_space=pl.ANY)] * 4,
        scratch_shapes=[
            vm((H, W, D), BF), vm((H, W, D), BF), vm((H, T, D), BF), vm((H, T, D), BF),
            vm((H, B, D), BF), vm((H, 8, B, D), BF), vm((H, 2, NF, B, D), BF),
            vm((H, T, D), BF), vm((H, T, D), BF), vm((H, T, D), F32), vm((H, T, D), F32),
            vm((H, T, D), BF), vm((H, T, D), BF), vm((2, H, EDGE, D), BF), vm((2, H, EDGE, D), BF),
            vm((H, 2, NF, B, D), BF), vm((H, NF, B, D), BF), vm((H, NF, B, D), BF),
            vm((H, 3, 3, B, D), BF), vm((H, 8, B, D), BF), vm((H, 8, B, D), BF),
            vm((16, T), F32), vm((NF, B, T), F32), vm((NW, B, 512), F32), vm((NF, B, T), BF), vm((NW, B, 512), BF),
            vm((1, T), F32), vm((1, T), F32), vm((D, T), F32), vm((D, T), F32),
            vm((D, T), BF), vm((T, D), BF), vm((1, T), F32), vm((D, T), BF),
            dma((4, H)), dma((4, H)), dma((2, H)), dma((2, H)), dma((H,)), dma((H,)), dma((H,)), dma((H,)),
            dma((H,)), dma((H,)),
            dma((4, H)), dma((4, H)), dma((H,)), dma((H,)), dma((H,)), dma((H,)), dma((H,)), dma((H,)),
            dma((2, H)), dma((2, H)),
        ],
        compiler_params=pltpu.CompilerParams(
            collective_id=0, has_side_effects=True, vmem_limit_bytes=58 * 1024 * 1024
        ),
    )(keys, values, queries, grad_out, pattern.T)
    return finish(results)


def solution(mesh):
    split = P(("ctx", "head"), None)
    return jax.shard_map(
        per_device, mesh=mesh, in_specs=(split,) * 4 + (P(),), out_specs=(split,) * 4, check_vma=False
    )
```

```python
import functools
import math

import jax
import jax.numpy as jnp
from jax import lax
from jax.experimental import pallas as pl
from jax.experimental.pallas import tpu as pltpu
from jax.sharding import PartitionSpec as P

D = 128
B = 128
NB = 6
NF = 12
EDGE = 384
T = 768
W = 1152
R = 192
H = 4
Z = 4
F32 = jnp.float32
BF = jnp.bfloat16
SCALE = 1.0 / math.sqrt(D)
C2 = math.log2(math.e) / math.sqrt(D)
MESH = pl.DeviceIdType.MESH
KV = (0, 1)
QG = (2, 3)


def tn(a, b):
    return lax.dot_general(a, b, (((0,), (0,)), ((), ())), preferred_element_type=F32)


def nn(a, b):
    return jnp.dot(a, b, preferred_element_type=F32)


def kernel(
    k_in, v_in, q_in, g_in, pat,
    o_out, dq_out, dk_out, dv_out,
    kb, vb, qb, gb, slot, rows, pool,
    ob, dqb, dkw, dvw, dkb, dvb, back_s, back_r,
    dpool, sib_r, pair, x_r, ysl, y_r,
    fb, sf, sn, ef, en, m_s, l_s, ot_s, dqt_s, gt_s, gs_s, de_s, qt_s, df, pm,
    a_s, a_r, h_s, h_r, y1_s, y1_r, x1_s, x1_r, s2_s, s2_r,
    o_s, o_r, gs_sd, gs_rc, gx_s, gx_rc, gy_s, gy_rc, b_s, b_r,
):
    ctx = lax.axis_index("ctx")
    z = lax.axis_index("head")
    c = ctx % 2
    y = (ctx // 2) % 4
    x = ctx // 8
    sib = ctx + 1 - 2 * c
    up = (ctx + 1) % 32
    down = (ctx + 31) % 32

    def xpeer(d):
        return ((x + d) % 4) * 8 + y * 2 + c

    def rowpeer(d, other):
        return ((y + d) % 4) * 2 + (1 - c if other else c)

    row_moves = [(d, other) for other in (0, 1) for d in (2, 1, 3)] + [(0, 1)]
    me8 = y * 2 + c

    def at(ctx_, z_):
        return {"ctx": ctx_, "head": z_}

    def remote(src, dst, ss, rs, dev):
        return pltpu.make_async_remote_copy(
            src_ref=src, dst_ref=dst, send_sem=ss, recv_sem=rs, device_id=dev, device_id_type=MESH
        )

    def done(ref, sem):
        pltpu.make_async_copy(ref, ref, sem).wait()

    barrier = pltpu.get_barrier_semaphore()
    peers = [at(ctx, (z + d) % Z) for d in (1, 2, 3)]
    peers += [at(x * 8 + rowpeer(*m), z) for m in row_moves] + [at(xpeer(d), z) for d in (1, 2, 3)]
    peers += [at(up, z), at(down, z)]
    for dev in peers:
        pl.semaphore_signal(barrier, inc=1, device_id=dev, device_id_type=MESH)

    phase = pat[4, NB * 32 - 1] % 16
    own = (phase - ctx * NB + 192) % 16
    ids = phase + 16 * lax.broadcasted_iota(jnp.int32, (16, B), 0)
    for b in range(NB):
        hit = jnp.full((16, B), jnp.inf, F32)
        for s in range(NF):
            hit = jnp.where(ids == pat[4 + s, ctx * NB + b], 0.0, hit)
        fb[:, b * B:(b + 1) * B] = hit

    @pl.when(ctx == 0)
    def _():
        kb[:, :EDGE, :] = jnp.zeros((H, EDGE, D), BF)
        vb[:, :EDGE, :] = jnp.zeros((H, EDGE, D), BF)

    @pl.when(ctx == 31)
    def _():
        back_r[...] = jnp.zeros((2, H, EDGE, D), BF)

    pl.semaphore_wait(barrier, len(peers))

    arrays = ((k_in, kb, EDGE), (v_in, vb, EDGE), (q_in, qb, 0), (g_in, gb, 0))

    def lanes(group, h):
        return pl.ds(pl.multiple_of((group * H + h) * D, D), D)

    def a_start(h, which):
        for n in which:
            src, dst, base = arrays[n]
            place = dst.at[h, pl.ds(pl.multiple_of(base + z * R, 64), R), :]
            for d in (2, 1, 3):
                to = (z + d) % Z
                remote(src.at[:, lanes(to, h)], place, a_s.at[n, h], a_r.at[n, h], at(ctx, to)).start()
            pltpu.make_async_copy(src.at[:, lanes(z, h)], place, a_r.at[n, h]).start()

    def b_stage(h):
        done(kb.at[h, EDGE:, :], a_r.at[0, h])
        done(vb.at[h, EDGE:, :], a_r.at[1, h])

        @pl.when(ctx < 31)
        def _():
            remote(kb.at[h, W - EDGE:, :], kb.at[h, :EDGE, :], h_s.at[0, h], h_r.at[0, h], at(up, z)).start()
            remote(vb.at[h, W - EDGE:, :], vb.at[h, :EDGE, :], h_s.at[1, h], h_r.at[1, h], at(up, z)).start()

        ks = jnp.zeros((B, D), BF)
        vs = jnp.zeros((B, D), BF)
        for b in range(NB):
            r = slice(EDGE + b * B, EDGE + (b + 1) * B)
            ks = jnp.where(own == b, kb[h, r, :], ks)
            vs = jnp.where(own == b, vb[h, r, :], vs)
        rows[h, me8] = jnp.where(c == 0, ks, vs)
        slot[h] = jnp.where(c == 0, vs, ks)
        for d, other in row_moves:
            src = slot.at[h] if other else rows.at[h, me8]
            to = at(x * 8 + rowpeer(d, other), z)
            remote(src, rows.at[h, me8], y1_s.at[h], y1_r.at[h], to).start()

    def d_stage(h):
        done(rows.at[h, :7], y1_r.at[h])
        for j in range(3):
            place = (phase + 16 * j) // NB
            blk = jnp.zeros((B, D), BF)
            for s in range(3 * j if j < 2 else 5, (3, 6, 8)[j]):
                blk = jnp.where(place == s, rows[h, s], blk)
            if j == 1:
                blk = jnp.where(place == 2, rows[h, 2], blk)
            pool[h, c, 3 * x + j] = blk
        mine = pool.at[h, c, pl.ds(3 * x, 3)]
        for d in (2, 1, 3):
            remote(mine, mine, x1_s.at[h], x1_r.at[h], at(xpeer(d), z)).start()

    def e_stage(h):
        done(pool.at[h, c, :9], x1_r.at[h])
        remote(pool.at[h, c], pool.at[h, c], s2_s.at[h], s2_r.at[h], at(sib, z)).start()

    def f_stage(h):
        done(qb.at[h], a_r.at[2, h])
        done(gb.at[h], a_r.at[3, h])

        @pl.when(ctx > 0)
        def _():
            done(kb.at[h, :EDGE, :], h_r.at[0, h])
            done(vb.at[h, :EDGE, :], h_r.at[1, h])

    def f2_stage(h):
        done(pool.at[h, 0], s2_r.at[h])

    def pair_cols(p):
        return slice(p * 256, p * 256 + 256)

    def pair_rows(p):
        return slice(p * 256, p * 256 + 640)

    def masks():
        key = lax.broadcasted_iota(jnp.int32, (640, 256), 0)
        query = lax.broadcasted_iota(jnp.int32, (640, 256), 1)
        first = jnp.where(ctx == 0, EDGE, 0)
        window = (key >= (query // B) * B) & (key <= query + EDGE)
        for p in range(3):
            pm[p] = jnp.where(window & (key + p * 256 >= first), 0.0, -jnp.inf)

    def near1(h):
        qt_s[...] = qb[h].T
        for p in range(3):
            s = nn(kb[h, pair_rows(p), :], qt_s[:, pair_cols(p)]) + pm[p]
            sn[p] = s
            m_s[:, pair_cols(p)] = jnp.max(s, axis=0, keepdims=True)

    def far1(h):
        top = jnp.full((8, T), -jnp.inf, F32)
        for i in range(NF):
            s = nn(pool[h, 0, i], qt_s[...])
            sf[i] = s
            top = jnp.maximum(top, jnp.max(s.reshape(16, 8, T), axis=0) - fb[i:i + 1, :])
        m_s[...] = jnp.maximum(m_s[...], jnp.max(top, axis=0, keepdims=True))

    def pass2(h):
        m = m_s[...]
        total = jnp.zeros((8, T), F32)
        for i in range(NF):
            e = jnp.exp2((sf[i] - (m + fb[i:i + 1, :])) * C2)
            total = total + jnp.sum(e.reshape(16, 8, T), axis=0)
            ef[i] = e.astype(BF)
        l_s[...] = jnp.sum(total, axis=0, keepdims=True)
        ot_s[...] = tn(pool[h, 1].reshape(NF * B, D), ef[...].reshape(NF * B, T))
        for p in range(3):
            cols = pair_cols(p)
            e = jnp.exp2((sn[p] - m[:, cols]) * C2)
            l_s[:, cols] += jnp.sum(e, axis=0, keepdims=True)
            e = e.astype(BF)
            en[p] = e
            ot_s[:, cols] += tn(vb[h, pair_rows(p), :], e)
        inv = 1.0 / l_s[...]
        ot = ot_s[...] * inv
        ob[h] = ot.T.astype(BF)
        gt = (gb[h].T.astype(F32) * inv).astype(BF)
        gt_s[...] = gt
        gs_s[...] = gt.T
        de_s[...] = jnp.sum(gt.astype(F32) * ot, axis=0, keepdims=True)

    def far3(h):
        sf[...] = nn(pool[h, 1].reshape(NF * B, D), gt_s[...]).reshape(NF, B, T)
        for i in range(NF):
            df[i] = (ef[i].astype(F32) * (sf[i] - de_s[...])).astype(BF)
        dpool[h, 1] = nn(ef[...].reshape(NF * B, T), gs_s[...]).astype(BF).reshape(NF, B, D)
        dpool[h, 0] = (nn(df[...].reshape(NF * B, T), qb[h]) * SCALE).astype(BF).reshape(NF, B, D)

    def near3(h):
        dqt_s[...] = tn(pool[h, 0].reshape(NF * B, D), df[...].reshape(NF * B, T))
        dkw[h] = jnp.zeros((W, D), F32)
        dvw[h] = jnp.zeros((W, D), F32)
        for p in range(3):
            cols, r = pair_cols(p), pair_rows(p)
            e = en[p]
            dvw[h, r, :] += nn(e, gs_s[cols, :])
            dp = nn(vb[h, r, :], gt_s[:, cols])
            ds = (e.astype(F32) * (dp - de_s[:, cols])).astype(BF)
            dkw[h, r, :] += nn(ds, qb[h, cols, :]) * SCALE
            dqt_s[:, cols] += tn(kb[h, r, :], ds)
        back_s[0, h] = dkw[h, :EDGE, :].astype(BF)
        back_s[1, h] = dvw[h, :EDGE, :].astype(BF)
        dqb[h] = (dqt_s[...].T * SCALE).astype(BF)

    outs = ((ob, o_out), (dqb, dq_out), (dkb, dk_out), (dvb, dv_out))

    def o_start(n, h):
        src, dst = outs[n]
        place = dst.at[:, lanes(z, h)]
        for d in (2, 1, 3):
            to = (z + d) % Z
            part = src.at[h, pl.ds(pl.multiple_of(to * R, 64), R), :]
            remote(part, place, o_s.at[n, h], o_r.at[n, h], at(ctx, to)).start()
        part = src.at[h, pl.ds(pl.multiple_of(z * R, 64), R), :]
        pltpu.make_async_copy(part, place, o_r.at[n, h]).start()

    def sib_send(h):
        remote(dpool.at[h, 1 - c], sib_r.at[h], gs_sd.at[h], gs_rc.at[h], at(sib, z)).start()

    def g0(h):
        @pl.when(ctx > 0)
        def _():
            for n in range(2):
                remote(back_s.at[n, h], back_r.at[n, h], b_s.at[n, h], b_r.at[n, h], at(down, z)).start()

        o_start(1, h)

    def g1(h):
        done(sib_r.at[h], gs_rc.at[h])
        for i in range(NF):
            pair[h, i] = (dpool[h, c, i].astype(F32) + sib_r[h, i].astype(F32)).astype(BF)
        for d in (2, 1, 3):
            to = (x + d) % 4
            remote(pair.at[h, pl.ds(3 * to, 3)], x_r.at[h, d - 1], gx_s.at[h], gx_rc.at[h], at(xpeer(d), z)).start()

    def g2(h):
        done(x_r.at[h], gx_rc.at[h])
        tot = []
        for j in range(3):
            t = pair[h, 3 * x + j].astype(F32)
            for d in range(3):
                t = t + x_r[h, d, j].astype(F32)
            tot.append(t)
        for s in range(8):
            t = jnp.zeros((B, D), F32)
            for j in range(3):
                if 16 * j <= s * NB + 5 and s * NB <= 16 * j + 15:
                    t = jnp.where((phase + 16 * j) // NB == s, tot[j], t)
            ysl[h, s] = t.astype(BF)
        for d, other in row_moves:
            to = rowpeer(d, other)
            remote(ysl.at[h, to], y_r.at[h, me8], gy_s.at[h], gy_rc.at[h], at(x * 8 + to, z)).start()
        y_r[h, me8] = ysl[h, me8]

    def g3(h):
        done(y_r.at[h, :7], gy_rc.at[h])

        @pl.when(ctx < 31)
        def _():
            done(back_r.at[0, h], b_r.at[0, h])
            done(back_r.at[1, h], b_r.at[1, h])

        for n, (part, total, dst) in enumerate(
            ((y_r, dkw, dkb), (y_r, dvw, dvb))
        ):
            part = part[h, n].astype(F32) + part[h, 2 + n].astype(F32) + part[h, 4 + n].astype(F32) + part[h, 6 + n].astype(F32)
            for b in range(NB):
                r = slice(b * B, (b + 1) * B)
                t = total[h, EDGE + b * B:EDGE + (b + 1) * B, :] + jnp.where(own == b, part, 0.0)
                if b >= 3:
                    t = t + back_r[n, h, (b - 3) * B:(b - 2) * B, :].astype(F32)
                dst[h, r, :] = t.astype(BF)
        o_start(2, h)
        o_start(3, h)

    for h, which in ((0, KV), (1, KV), (2, KV), (0, QG), (3, KV), (1, QG), (2, QG), (3, QG)):
        a_start(h, which)
    masks()
    b_stage(0)
    b_stage(1)
    d_stage(0)
    b_stage(2)
    d_stage(1)
    e_stage(0)
    d_stage(2)

    @pl.loop(0, H)
    def _(t):
        f_stage(t)
        near1(t)

        @pl.when(t >= 1)
        def _():
            g1(t - 1)

        f2_stage(t)
        far1(t)

        @pl.when(t == 0)
        def _():
            b_stage(3)

        @pl.when(t + 1 < H)
        def _():
            e_stage(t + 1)

        @pl.when(t >= 2)
        def _():
            g3(t - 2)

        pass2(t)
        o_start(0, t)
        far3(t)
        sib_send(t)

        @pl.when(t == 0)
        def _():
            d_stage(3)

        @pl.when(t >= 1)
        def _():
            g2(t - 1)

        near3(t)
        g0(t)

    g1(H - 1)
    g3(H - 2)
    g2(H - 1)
    g3(H - 1)

    @pl.loop(0, H)
    def _(h):
        for n in range(4):
            done(qb.at[h, :3 * R, :], a_s.at[n, h])
            done(qb.at[h, :3 * R, :], o_s.at[n, h])
            done(qb.at[h], o_r.at[n, h])
        done(rows.at[h, :7], y1_s.at[h])
        done(pool.at[h, 0, :9], x1_s.at[h])
        done(pool.at[h, 0], s2_s.at[h])
        done(sib_r.at[h], gs_sd.at[h])
        done(x_r.at[h], gx_s.at[h])
        done(y_r.at[h, :7], gy_s.at[h])

        @pl.when(ctx < 31)
        def _():
            done(back_r.at[0, h], h_s.at[0, h])
            done(back_r.at[0, h], h_s.at[1, h])

        @pl.when(ctx > 0)
        def _():
            done(back_r.at[0, h], b_s.at[0, h])
            done(back_r.at[0, h], b_s.at[1, h])


def settle(*refs):
    src, dst, held, in_sem, out_sem = refs[:4], refs[4:8], refs[8], refs[9], refs[10]
    half = R // 2
    parts = [(n, slice(m * half, (m + 1) * half), 2 * n + m) for n in range(4) for m in range(2)]
    ins = [pltpu.make_async_copy(src[n].at[r], held.at[n, r], in_sem.at[i]) for n, r, i in parts]
    outs = [pltpu.make_async_copy(held.at[n, r], dst[n].at[r], out_sem.at[i]) for n, r, i in parts]
    for copy in ins:
        copy.start()
    for first, second in zip(ins, outs):
        first.wait()
        second.start()
    for copy in outs:
        copy.wait()


def finish(results):
    return pl.pallas_call(
        settle,
        out_shape=[jax.ShapeDtypeStruct((R, H * Z * D), BF)] * 4,
        in_specs=[pl.BlockSpec(memory_space=pl.ANY)] * 4,
        out_specs=[pl.BlockSpec(memory_space=pl.ANY)] * 4,
        scratch_shapes=[
            pltpu.VMEM((4, R, H * Z * D), BF),
            pltpu.SemaphoreType.DMA((8,)),
            pltpu.SemaphoreType.DMA((8,)),
        ],
        compiler_params=pltpu.CompilerParams(vmem_limit_bytes=58 * 1024 * 1024),
    )(*results)


def per_device(queries, keys, values, grad_out, pattern):
    vm = pltpu.VMEM
    dma = pltpu.SemaphoreType.DMA
    results = pl.pallas_call(
        kernel,
        out_shape=[jax.ShapeDtypeStruct((R, H * Z * D), BF)] * 4,
        in_specs=[pl.BlockSpec(memory_space=pl.ANY)] * 4 + [pl.BlockSpec(memory_space=pltpu.SMEM)],
        out_specs=[pl.BlockSpec(memory_space=pl.ANY)] * 4,
        scratch_shapes=[
            vm((H, W, D), BF), vm((H, W, D), BF), vm((H, T, D), BF), vm((H, T, D), BF),
            vm((H, B, D), BF), vm((H, 8, B, D), BF), vm((H, 2, NF, B, D), BF),
            vm((H, T, D), BF), vm((H, T, D), BF), vm((H, W, D), F32), vm((H, W, D), F32),
            vm((H, T, D), BF), vm((H, T, D), BF), vm((2, H, EDGE, D), BF), vm((2, H, EDGE, D), BF),
            vm((H, 2, NF, B, D), BF), vm((H, NF, B, D), BF), vm((H, NF, B, D), BF),
            vm((H, 3, 3, B, D), BF), vm((H, 8, B, D), BF), vm((H, 8, B, D), BF),
            vm((16, T), F32), vm((NF, B, T), F32), vm((3, 640, 256), F32), vm((NF, B, T), BF), vm((3, 640, 256), BF),
            vm((1, T), F32), vm((1, T), F32), vm((D, T), F32), vm((D, T), F32),
            vm((D, T), BF), vm((T, D), BF), vm((1, T), F32), vm((D, T), BF),
            vm((NF, B, T), BF), vm((3, 640, 256), F32),
            dma((4, H)), dma((4, H)), dma((2, H)), dma((2, H)), dma((H,)), dma((H,)), dma((H,)), dma((H,)),
            dma((H,)), dma((H,)),
            dma((4, H)), dma((4, H)), dma((H,)), dma((H,)), dma((H,)), dma((H,)), dma((H,)), dma((H,)),
            dma((2, H)), dma((2, H)),
        ],
        compiler_params=pltpu.CompilerParams(
            collective_id=0, has_side_effects=True, vmem_limit_bytes=58 * 1024 * 1024
        ),
    )(keys, values, queries, grad_out, pattern.T)
    return finish(results)


def solution(mesh):
    split = P(("ctx", "head"), None)
    return jax.shard_map(
        per_device, mesh=mesh, in_specs=(split,) * 4 + (P(),), out_specs=(split,) * 4, check_vma=False
    )
```

```python
import functools
import math

import jax
import jax.numpy as jnp
from jax import lax
from jax.experimental import pallas as pl
from jax.experimental.pallas import tpu as pltpu
from jax.sharding import PartitionSpec as P

D = 128
B = 128
NB = 6
NF = 12
EDGE = 384
T = 768
W = 1152
R = 192
H = 4
Z = 4
F32 = jnp.float32
BF = jnp.bfloat16
SCALE = 1.0 / math.sqrt(D)
C2 = math.log2(math.e) / math.sqrt(D)
MESH = pl.DeviceIdType.MESH
KV = (0, 1)
QG = (2, 3)


def tn(a, b):
    return lax.dot_general(a, b, (((0,), (0,)), ((), ())), preferred_element_type=F32)


def nn(a, b):
    return jnp.dot(a, b, preferred_element_type=F32)


def kernel(
    k_in, v_in, q_in, g_in, pat,
    o_out, dq_out, dk_out, dv_out,
    kb, vb, qb, gb, slot, rows, pool,
    ob, dqb, dkw, dvw, dkb, dvb, back_s, back_r,
    dpool, sib_r, pair, x_r, ysl, y_r,
    fb, sf, sn, ef, en, m_s, l_s, ot_s, dqt_s, gt_s, gs_s, de_s, qt_s, df, pm,
    a_s, a_r, h_s, h_r, y1_s, y1_r, x1_s, x1_r, s2_s, s2_r,
    o_s, o_r, gs_sd, gs_rc, gx_s, gx_rc, gy_s, gy_rc, b_s, b_r,
):
    ctx = lax.axis_index("ctx")
    z = lax.axis_index("head")
    c = ctx % 2
    y = (ctx // 2) % 4
    x = ctx // 8
    sib = ctx + 1 - 2 * c
    up = (ctx + 1) % 32
    down = (ctx + 31) % 32

    def xpeer(d):
        return ((x + d) % 4) * 8 + y * 2 + c

    def rowpeer(d, other):
        return ((y + d) % 4) * 2 + (1 - c if other else c)

    row_moves = [(d, other) for other in (0, 1) for d in (2, 1, 3)] + [(0, 1)]
    me8 = y * 2 + c

    def at(ctx_, z_):
        return {"ctx": ctx_, "head": z_}

    def remote(src, dst, ss, rs, dev):
        return pltpu.make_async_remote_copy(
            src_ref=src, dst_ref=dst, send_sem=ss, recv_sem=rs, device_id=dev, device_id_type=MESH
        )

    def done(ref, sem):
        pltpu.make_async_copy(ref, ref, sem).wait()

    barrier = pltpu.get_barrier_semaphore()
    peers = [at(ctx, (z + d) % Z) for d in (1, 2, 3)]
    peers += [at(x * 8 + rowpeer(*m), z) for m in row_moves] + [at(xpeer(d), z) for d in (1, 2, 3)]
    peers += [at(up, z), at(down, z)]
    for dev in peers:
        pl.semaphore_signal(barrier, inc=1, device_id=dev, device_id_type=MESH)

    phase = pat[4, NB * 32 - 1] % 16
    own = (phase - ctx * NB + 192) % 16
    ids = phase + 16 * lax.broadcasted_iota(jnp.int32, (16, B), 0)
    for b in range(NB):
        hit = jnp.full((16, B), jnp.inf, F32)
        for s in range(NF):
            hit = jnp.where(ids == pat[4 + s, ctx * NB + b], 0.0, hit)
        fb[:, b * B:(b + 1) * B] = hit

    @pl.when(ctx == 0)
    def _():
        kb[:, :EDGE, :] = jnp.zeros((H, EDGE, D), BF)
        vb[:, :EDGE, :] = jnp.zeros((H, EDGE, D), BF)

    @pl.when(ctx == 31)
    def _():
        back_r[...] = jnp.zeros((2, H, EDGE, D), BF)

    pl.semaphore_wait(barrier, len(peers))

    arrays = ((k_in, kb, EDGE), (v_in, vb, EDGE), (q_in, qb, 0), (g_in, gb, 0))

    def lanes(group, h):
        return pl.ds(pl.multiple_of((group * H + h) * D, D), D)

    def a_start(h, which):
        for n in which:
            src, dst, base = arrays[n]
            place = dst.at[h, pl.ds(pl.multiple_of(base + z * R, 64), R), :]
            for d in (2, 1, 3):
                to = (z + d) % Z
                remote(src.at[:, lanes(to, h)], place, a_s.at[n, h], a_r.at[n, h], at(ctx, to)).start()
            pltpu.make_async_copy(src.at[:, lanes(z, h)], place, a_r.at[n, h]).start()

    def b_stage(h):
        done(kb.at[h, EDGE:, :], a_r.at[0, h])
        done(vb.at[h, EDGE:, :], a_r.at[1, h])

        @pl.when(ctx < 31)
        def _():
            remote(kb.at[h, W - EDGE:, :], kb.at[h, :EDGE, :], h_s.at[0, h], h_r.at[0, h], at(up, z)).start()
            remote(vb.at[h, W - EDGE:, :], vb.at[h, :EDGE, :], h_s.at[1, h], h_r.at[1, h], at(up, z)).start()

        ks = jnp.zeros((B, D), BF)
        vs = jnp.zeros((B, D), BF)
        for b in range(NB):
            r = slice(EDGE + b * B, EDGE + (b + 1) * B)
            ks = jnp.where(own == b, kb[h, r, :], ks)
            vs = jnp.where(own == b, vb[h, r, :], vs)
        rows[h, me8] = jnp.where(c == 0, ks, vs)
        slot[h] = jnp.where(c == 0, vs, ks)
        for d, other in row_moves:
            src = slot.at[h] if other else rows.at[h, me8]
            to = at(x * 8 + rowpeer(d, other), z)
            remote(src, rows.at[h, me8], y1_s.at[h], y1_r.at[h], to).start()

    def d_stage(h):
        done(rows.at[h, :7], y1_r.at[h])
        for j in range(3):
            place = (phase + 16 * j) // NB
            blk = jnp.zeros((B, D), BF)
            for s in range(3 * j if j < 2 else 5, (3, 6, 8)[j]):
                blk = jnp.where(place == s, rows[h, s], blk)
            if j == 1:
                blk = jnp.where(place == 2, rows[h, 2], blk)
            pool[h, c, 3 * x + j] = blk
        mine = pool.at[h, c, pl.ds(3 * x, 3)]
        for d in (2, 1, 3):
            remote(mine, mine, x1_s.at[h], x1_r.at[h], at(xpeer(d), z)).start()

    def e_stage(h):
        done(pool.at[h, c, :9], x1_r.at[h])
        remote(pool.at[h, c], pool.at[h, c], s2_s.at[h], s2_r.at[h], at(sib, z)).start()

    def f_stage(h):
        done(qb.at[h], a_r.at[2, h])
        done(gb.at[h], a_r.at[3, h])

        @pl.when(ctx > 0)
        def _():
            done(kb.at[h, :EDGE, :], h_r.at[0, h])
            done(vb.at[h, :EDGE, :], h_r.at[1, h])

    def f2_stage(h):
        done(pool.at[h, 0], s2_r.at[h])

    def pair_cols(p):
        return slice(p * 256, p * 256 + 256)

    def pair_rows(p):
        return slice(p * 256, p * 256 + 640)

    def masks():
        key = lax.broadcasted_iota(jnp.int32, (640, 256), 0)
        query = lax.broadcasted_iota(jnp.int32, (640, 256), 1)
        first = jnp.where(ctx == 0, EDGE, 0)
        window = (key >= (query // B) * B) & (key <= query + EDGE)
        for p in range(3):
            pm[p] = jnp.where(window & (key + p * 256 >= first), 0.0, -jnp.inf)

    def near1(h):
        qt_s[...] = qb[h].T
        for p in range(3):
            s = nn(kb[h, pair_rows(p), :], qt_s[:, pair_cols(p)]) + pm[p]
            sn[p] = s
            m_s[:, pair_cols(p)] = jnp.max(s, axis=0, keepdims=True)

    def far1(h):
        top = jnp.full((8, T), -jnp.inf, F32)
        for i in range(NF):
            s = nn(pool[h, 0, i], qt_s[...])
            sf[i] = s
            top = jnp.maximum(top, jnp.max(s.reshape(16, 8, T), axis=0) - fb[i:i + 1, :])
        m_s[...] = jnp.maximum(m_s[...], jnp.max(top, axis=0, keepdims=True))

    def pass2(h):
        m = m_s[...]
        total = jnp.zeros((8, T), F32)
        for i in range(NF):
            e = jnp.exp2((sf[i] - (m + fb[i:i + 1, :])) * C2)
            total = total + jnp.sum(e.reshape(16, 8, T), axis=0)
            ef[i] = e.astype(BF)
        l_s[...] = jnp.sum(total, axis=0, keepdims=True)
        ot_s[...] = tn(pool[h, 1].reshape(NF * B, D), ef[...].reshape(NF * B, T))
        for p in range(3):
            cols = pair_cols(p)
            e = jnp.exp2((sn[p] - m[:, cols]) * C2)
            l_s[:, cols] += jnp.sum(e, axis=0, keepdims=True)
            e = e.astype(BF)
            en[p] = e
            ot_s[:, cols] += tn(vb[h, pair_rows(p), :], e)
        inv = 1.0 / l_s[...]
        ot = ot_s[...] * inv
        ob[h] = ot.T.astype(BF)
        gt = (gb[h].T.astype(F32) * inv).astype(BF)
        gt_s[...] = gt
        gs_s[...] = gt.T
        de_s[...] = jnp.sum(gt.astype(F32) * ot, axis=0, keepdims=True)

    def far3(h):
        sf[...] = nn(pool[h, 1].reshape(NF * B, D), gt_s[...]).reshape(NF, B, T)
        for i in range(NF):
            df[i] = (ef[i].astype(F32) * (sf[i] - de_s[...])).astype(BF)
        dpool[h, 1] = nn(ef[...].reshape(NF * B, T), gs_s[...]).astype(BF).reshape(NF, B, D)
        dpool[h, 0] = (nn(df[...].reshape(NF * B, T), qb[h]) * SCALE).astype(BF).reshape(NF, B, D)

    def near3(h):
        dqt_s[...] = tn(pool[h, 0].reshape(NF * B, D), df[...].reshape(NF * B, T))
        dkw[h] = jnp.zeros((W, D), F32)
        dvw[h] = jnp.zeros((W, D), F32)
        for p in range(3):
            cols, r = pair_cols(p), pair_rows(p)
            e = en[p]
            dvw[h, r, :] += nn(e, gs_s[cols, :])
            dp = nn(vb[h, r, :], gt_s[:, cols])
            ds = (e.astype(F32) * (dp - de_s[:, cols])).astype(BF)
            dkw[h, r, :] += nn(ds, qb[h, cols, :]) * SCALE
            dqt_s[:, cols] += tn(kb[h, r, :], ds)
        back_s[0, h] = dkw[h, :EDGE, :].astype(BF)
        back_s[1, h] = dvw[h, :EDGE, :].astype(BF)
        dqb[h] = (dqt_s[...].T * SCALE).astype(BF)

    outs = ((ob, o_out), (dqb, dq_out), (dkb, dk_out), (dvb, dv_out))

    def o_start(n, h):
        src, dst = outs[n]
        place = dst.at[:, lanes(z, h)]
        for d in (2, 1, 3):
            to = (z + d) % Z
            part = src.at[h, pl.ds(pl.multiple_of(to * R, 64), R), :]
            remote(part, place, o_s.at[n, h], o_r.at[n, h], at(ctx, to)).start()
        part = src.at[h, pl.ds(pl.multiple_of(z * R, 64), R), :]
        pltpu.make_async_copy(part, place, o_r.at[n, h]).start()

    def sib_send(h):
        remote(dpool.at[h, 1 - c], sib_r.at[h], gs_sd.at[h], gs_rc.at[h], at(sib, z)).start()

    def g0(h):
        @pl.when(ctx > 0)
        def _():
            for n in range(2):
                remote(back_s.at[n, h], back_r.at[n, h], b_s.at[n, h], b_r.at[n, h], at(down, z)).start()

        o_start(1, h)

    def g1(h):
        done(sib_r.at[h], gs_rc.at[h])
        for i in range(NF):
            pair[h, i] = (dpool[h, c, i].astype(F32) + sib_r[h, i].astype(F32)).astype(BF)
        for d in (2, 1, 3):
            to = (x + d) % 4
            remote(pair.at[h, pl.ds(3 * to, 3)], x_r.at[h, d - 1], gx_s.at[h], gx_rc.at[h], at(xpeer(d), z)).start()

    def g2(h):
        done(x_r.at[h], gx_rc.at[h])
        tot = []
        for j in range(3):
            t = pair[h, 3 * x + j].astype(F32)
            for d in range(3):
                t = t + x_r[h, d, j].astype(F32)
            tot.append(t)
        for s in range(8):
            t = jnp.zeros((B, D), F32)
            for j in range(3):
                if 16 * j <= s * NB + 5 and s * NB <= 16 * j + 15:
                    t = jnp.where((phase + 16 * j) // NB == s, tot[j], t)
            ysl[h, s] = t.astype(BF)
        for d, other in row_moves:
            to = rowpeer(d, other)
            remote(ysl.at[h, to], y_r.at[h, me8], gy_s.at[h], gy_rc.at[h], at(x * 8 + to, z)).start()
        y_r[h, me8] = ysl[h, me8]

    def g3(h):
        done(y_r.at[h, :7], gy_rc.at[h])

        @pl.when(ctx < 31)
        def _():
            done(back_r.at[0, h], b_r.at[0, h])
            done(back_r.at[1, h], b_r.at[1, h])

        for n, (part, total, dst) in enumerate(
            ((y_r, dkw, dkb), (y_r, dvw, dvb))
        ):
            part = part[h, n].astype(F32) + part[h, 2 + n].astype(F32) + part[h, 4 + n].astype(F32) + part[h, 6 + n].astype(F32)
            for b in range(NB):
                r = slice(b * B, (b + 1) * B)
                t = total[h, EDGE + b * B:EDGE + (b + 1) * B, :] + jnp.where(own == b, part, 0.0)
                if b >= 3:
                    t = t + back_r[n, h, (b - 3) * B:(b - 2) * B, :].astype(F32)
                dst[h, r, :] = t.astype(BF)
        o_start(2, h)
        o_start(3, h)

    for h, which in ((0, KV), (1, KV), (2, KV), (0, QG), (3, KV), (1, QG), (2, QG), (3, QG)):
        a_start(h, which)
    masks()
    b_stage(0)
    b_stage(1)
    d_stage(0)
    b_stage(2)
    d_stage(1)
    e_stage(0)

    @pl.loop(0, H)
    def _(t):
        f_stage(t)
        near1(t)

        @pl.when(t == 0)
        def _():
            d_stage(2)

        @pl.when(t >= 1)
        def _():
            g1(t - 1)

        f2_stage(t)
        far1(t)

        @pl.when(t == 0)
        def _():
            b_stage(3)

        @pl.when(t + 1 < H)
        def _():
            e_stage(t + 1)

        @pl.when(t >= 2)
        def _():
            g2(t - 2)

        @pl.when(t >= 3)
        def _():
            g3(t - 3)

        pass2(t)
        o_start(0, t)
        far3(t)
        sib_send(t)

        @pl.when(t == 0)
        def _():
            d_stage(3)

        near3(t)
        g0(t)

    g1(H - 1)
    g3(H - 3)
    g2(H - 2)
    g3(H - 2)
    g2(H - 1)
    g3(H - 1)

    @pl.loop(0, H)
    def _(h):
        for n in range(4):
            done(qb.at[h, :3 * R, :], a_s.at[n, h])
            done(qb.at[h, :3 * R, :], o_s.at[n, h])
            done(qb.at[h], o_r.at[n, h])
        done(rows.at[h, :7], y1_s.at[h])
        done(pool.at[h, 0, :9], x1_s.at[h])
        done(pool.at[h, 0], s2_s.at[h])
        done(sib_r.at[h], gs_sd.at[h])
        done(x_r.at[h], gx_s.at[h])
        done(y_r.at[h, :7], gy_s.at[h])

        @pl.when(ctx < 31)
        def _():
            done(back_r.at[0, h], h_s.at[0, h])
            done(back_r.at[0, h], h_s.at[1, h])

        @pl.when(ctx > 0)
        def _():
            done(back_r.at[0, h], b_s.at[0, h])
            done(back_r.at[0, h], b_s.at[1, h])


def settle(*refs):
    src, dst, held, in_sem, out_sem = refs[:4], refs[4:8], refs[8], refs[9], refs[10]
    half = R // 2
    parts = [(n, slice(m * half, (m + 1) * half), 2 * n + m) for n in range(4) for m in range(2)]
    ins = [pltpu.make_async_copy(src[n].at[r], held.at[n, r], in_sem.at[i]) for n, r, i in parts]
    outs = [pltpu.make_async_copy(held.at[n, r], dst[n].at[r], out_sem.at[i]) for n, r, i in parts]
    for copy in ins:
        copy.start()
    for first, second in zip(ins, outs):
        first.wait()
        second.start()
    for copy in outs:
        copy.wait()


def finish(results):
    return pl.pallas_call(
        settle,
        out_shape=[jax.ShapeDtypeStruct((R, H * Z * D), BF)] * 4,
        in_specs=[pl.BlockSpec(memory_space=pl.ANY)] * 4,
        out_specs=[pl.BlockSpec(memory_space=pl.ANY)] * 4,
        scratch_shapes=[
            pltpu.VMEM((4, R, H * Z * D), BF),
            pltpu.SemaphoreType.DMA((8,)),
            pltpu.SemaphoreType.DMA((8,)),
        ],
        compiler_params=pltpu.CompilerParams(vmem_limit_bytes=58 * 1024 * 1024),
    )(*results)


def per_device(queries, keys, values, grad_out, pattern):
    vm = pltpu.VMEM
    dma = pltpu.SemaphoreType.DMA
    results = pl.pallas_call(
        kernel,
        out_shape=[jax.ShapeDtypeStruct((R, H * Z * D), BF)] * 4,
        in_specs=[pl.BlockSpec(memory_space=pl.ANY)] * 4 + [pl.BlockSpec(memory_space=pltpu.SMEM)],
        out_specs=[pl.BlockSpec(memory_space=pl.ANY)] * 4,
        scratch_shapes=[
            vm((H, W, D), BF), vm((H, W, D), BF), vm((H, T, D), BF), vm((H, T, D), BF),
            vm((H, B, D), BF), vm((H, 8, B, D), BF), vm((H, 2, NF, B, D), BF),
            vm((H, T, D), BF), vm((H, T, D), BF), vm((H, W, D), F32), vm((H, W, D), F32),
            vm((H, T, D), BF), vm((H, T, D), BF), vm((2, H, EDGE, D), BF), vm((2, H, EDGE, D), BF),
            vm((H, 2, NF, B, D), BF), vm((H, NF, B, D), BF), vm((H, NF, B, D), BF),
            vm((H, 3, 3, B, D), BF), vm((H, 8, B, D), BF), vm((H, 8, B, D), BF),
            vm((16, T), F32), vm((NF, B, T), F32), vm((3, 640, 256), F32), vm((NF, B, T), BF), vm((3, 640, 256), BF),
            vm((1, T), F32), vm((1, T), F32), vm((D, T), F32), vm((D, T), F32),
            vm((D, T), BF), vm((T, D), BF), vm((1, T), F32), vm((D, T), BF),
            vm((NF, B, T), BF), vm((3, 640, 256), F32),
            dma((4, H)), dma((4, H)), dma((2, H)), dma((2, H)), dma((H,)), dma((H,)), dma((H,)), dma((H,)),
            dma((H,)), dma((H,)),
            dma((4, H)), dma((4, H)), dma((H,)), dma((H,)), dma((H,)), dma((H,)), dma((H,)), dma((H,)),
            dma((2, H)), dma((2, H)),
        ],
        compiler_params=pltpu.CompilerParams(
            collective_id=0, has_side_effects=True, vmem_limit_bytes=58 * 1024 * 1024
        ),
    )(keys, values, queries, grad_out, pattern.T)
    return finish(results)


def solution(mesh):
    split = P(("ctx", "head"), None)
    return jax.shard_map(
        per_device, mesh=mesh, in_specs=(split,) * 4 + (P(),), out_specs=(split,) * 4, check_vma=False
    )
```

```python
import functools
import math

import jax
import jax.numpy as jnp
from jax import lax
from jax.experimental import pallas as pl
from jax.experimental.pallas import tpu as pltpu
from jax.sharding import PartitionSpec as P

D = 128
B = 128
NB = 6
NF = 12
EDGE = 384
T = 768
W = 1152
R = 192
H = 4
Z = 4
F32 = jnp.float32
BF = jnp.bfloat16
SCALE = 1.0 / math.sqrt(D)
C2 = math.log2(math.e) / math.sqrt(D)
MESH = pl.DeviceIdType.MESH
KV = (0, 1)
QG = (2, 3)


def tn(a, b):
    return lax.dot_general(a, b, (((0,), (0,)), ((), ())), preferred_element_type=F32)


def nn(a, b):
    return jnp.dot(a, b, preferred_element_type=F32)


def kernel(
    k_in, v_in, q_in, g_in, pat,
    o_out, dq_out, dk_out, dv_out,
    kb, vb, qb, gb, slot, rows, pool,
    ob, dqb, dkw, dvw, dkb, dvb, back_s, back_r,
    dpool, sib_r, pair, x_r, ysl, y_r,
    fb, sf, sn, ef, en, m_s, l_s, ot_s, dqt_s, gt_s, gs_s, de_s, qt_s, df, pm,
    a_s, a_r, h_s, h_r, y1_s, y1_r, x1_s, x1_r, s2_s, s2_r,
    o_s, o_r, gs_sd, gs_rc, gx_s, gx_rc, gy_s, gy_rc, b_s, b_r,
):
    ctx = lax.axis_index("ctx")
    z = lax.axis_index("head")
    c = ctx % 2
    y = (ctx // 2) % 4
    x = ctx // 8
    sib = ctx + 1 - 2 * c
    up = (ctx + 1) % 32
    down = (ctx + 31) % 32

    def xpeer(d):
        return ((x + d) % 4) * 8 + y * 2 + c

    def rowpeer(d, other):
        return ((y + d) % 4) * 2 + (1 - c if other else c)

    row_moves = [(d, other) for other in (0, 1) for d in (2, 1, 3)] + [(0, 1)]
    me8 = y * 2 + c

    def at(ctx_, z_):
        return {"ctx": ctx_, "head": z_}

    def remote(src, dst, ss, rs, dev):
        return pltpu.make_async_remote_copy(
            src_ref=src, dst_ref=dst, send_sem=ss, recv_sem=rs, device_id=dev, device_id_type=MESH
        )

    def done(ref, sem):
        pltpu.make_async_copy(ref, ref, sem).wait()

    barrier = pltpu.get_barrier_semaphore()
    peers = [at(ctx, (z + d) % Z) for d in (1, 2, 3)]
    peers += [at(x * 8 + rowpeer(*m), z) for m in row_moves] + [at(xpeer(d), z) for d in (1, 2, 3)]
    peers += [at(up, z), at(down, z)]
    for dev in peers:
        pl.semaphore_signal(barrier, inc=1, device_id=dev, device_id_type=MESH)

    phase = pat[4, NB * 32 - 1] % 16
    own = (phase - ctx * NB + 192) % 16
    ids = phase + 16 * lax.broadcasted_iota(jnp.int32, (16, B), 0)
    for b in range(NB):
        hit = jnp.full((16, B), jnp.inf, F32)
        for s in range(NF):
            hit = jnp.where(ids == pat[4 + s, ctx * NB + b], 0.0, hit)
        fb[:, b * B:(b + 1) * B] = hit

    @pl.when(ctx == 0)
    def _():
        kb[:, :EDGE, :] = jnp.zeros((H, EDGE, D), BF)
        vb[:, :EDGE, :] = jnp.zeros((H, EDGE, D), BF)

    @pl.when(ctx == 31)
    def _():
        back_r[...] = jnp.zeros((2, H, EDGE, D), BF)

    pl.semaphore_wait(barrier, len(peers))

    arrays = ((k_in, kb, EDGE), (v_in, vb, EDGE), (q_in, qb, 0), (g_in, gb, 0))

    def lanes(group, h):
        return pl.ds(pl.multiple_of((group * H + h) * D, D), D)

    def a_start(h, which):
        for n in which:
            src, dst, base = arrays[n]
            place = dst.at[h, pl.ds(pl.multiple_of(base + z * R, 64), R), :]
            for d in (2, 1, 3):
                to = (z + d) % Z
                remote(src.at[:, lanes(to, h)], place, a_s.at[n, h], a_r.at[n, h], at(ctx, to)).start()
            pltpu.make_async_copy(src.at[:, lanes(z, h)], place, a_r.at[n, h]).start()

    def b_stage(h):
        done(kb.at[h, EDGE:, :], a_r.at[0, h])
        done(vb.at[h, EDGE:, :], a_r.at[1, h])

        @pl.when(ctx < 31)
        def _():
            remote(kb.at[h, W - EDGE:, :], kb.at[h, :EDGE, :], h_s.at[0, h], h_r.at[0, h], at(up, z)).start()
            remote(vb.at[h, W - EDGE:, :], vb.at[h, :EDGE, :], h_s.at[1, h], h_r.at[1, h], at(up, z)).start()

        ks = jnp.zeros((B, D), BF)
        vs = jnp.zeros((B, D), BF)
        for b in range(NB):
            r = slice(EDGE + b * B, EDGE + (b + 1) * B)
            ks = jnp.where(own == b, kb[h, r, :], ks)
            vs = jnp.where(own == b, vb[h, r, :], vs)
        rows[h, me8] = jnp.where(c == 0, ks, vs)
        slot[h] = jnp.where(c == 0, vs, ks)
        for d, other in row_moves:
            src = slot.at[h] if other else rows.at[h, me8]
            to = at(x * 8 + rowpeer(d, other), z)
            remote(src, rows.at[h, me8], y1_s.at[h], y1_r.at[h], to).start()

    def d_stage(h):
        done(rows.at[h, :7], y1_r.at[h])
        for j in range(3):
            place = (phase + 16 * j) // NB
            blk = jnp.zeros((B, D), BF)
            for s in range(3 * j if j < 2 else 5, (3, 6, 8)[j]):
                blk = jnp.where(place == s, rows[h, s], blk)
            if j == 1:
                blk = jnp.where(place == 2, rows[h, 2], blk)
            pool[h, c, 3 * x + j] = blk
        mine = pool.at[h, c, pl.ds(3 * x, 3)]
        for d in (2, 1, 3):
            remote(mine, mine, x1_s.at[h], x1_r.at[h], at(xpeer(d), z)).start()

    def e_stage(h):
        done(pool.at[h, c, :9], x1_r.at[h])
        remote(pool.at[h, c], pool.at[h, c], s2_s.at[h], s2_r.at[h], at(sib, z)).start()

    def f_stage(h):
        done(qb.at[h], a_r.at[2, h])
        done(gb.at[h], a_r.at[3, h])

        @pl.when(ctx > 0)
        def _():
            done(kb.at[h, :EDGE, :], h_r.at[0, h])
            done(vb.at[h, :EDGE, :], h_r.at[1, h])

    def f2_stage(h):
        done(pool.at[h, 0], s2_r.at[h])

    def pair_cols(p):
        return slice(p * 256, p * 256 + 256)

    def pair_rows(p):
        return slice(p * 256, p * 256 + 640)

    def masks():
        key = lax.broadcasted_iota(jnp.int32, (640, 256), 0)
        query = lax.broadcasted_iota(jnp.int32, (640, 256), 1)
        first = jnp.where(ctx == 0, EDGE, 0)
        window = (key >= (query // B) * B) & (key <= query + EDGE)
        for p in range(3):
            pm[p] = jnp.where(window & (key + p * 256 >= first), 0.0, -jnp.inf)

    def near1(h):
        qt_s[...] = qb[h].T
        for p in range(3):
            s = nn(kb[h, pair_rows(p), :], qt_s[:, pair_cols(p)]) + pm[p]
            sn[p] = s
            m_s[:, pair_cols(p)] = jnp.max(s, axis=0, keepdims=True)

    def far1(h):
        top = jnp.full((8, T), -jnp.inf, F32)
        for i in range(NF):
            s = nn(pool[h, 0, i], qt_s[...])
            sf[i] = s
            top = jnp.maximum(top, jnp.max(s.reshape(16, 8, T), axis=0) - fb[i:i + 1, :])
        m_s[...] = jnp.maximum(m_s[...], jnp.max(top, axis=0, keepdims=True))

    def pass2(h):
        m = m_s[...]
        total = jnp.zeros((8, T), F32)
        for i in range(NF):
            e = jnp.exp2((sf[i] - (m + fb[i:i + 1, :])) * C2)
            total = total + jnp.sum(e.reshape(16, 8, T), axis=0)
            ef[i] = e.astype(BF)
        l_s[...] = jnp.sum(total, axis=0, keepdims=True)
        ot_s[...] = tn(pool[h, 1].reshape(NF * B, D), ef[...].reshape(NF * B, T))
        for p in range(3):
            cols = pair_cols(p)
            e = jnp.exp2((sn[p] - m[:, cols]) * C2)
            l_s[:, cols] += jnp.sum(e, axis=0, keepdims=True)
            e = e.astype(BF)
            en[p] = e
            ot_s[:, cols] += tn(vb[h, pair_rows(p), :], e)
        inv = 1.0 / l_s[...]
        ot = ot_s[...] * inv
        ob[h] = ot.T.astype(BF)
        gt = (gb[h].T.astype(F32) * inv).astype(BF)
        gt_s[...] = gt
        gs_s[...] = gt.T
        de_s[...] = jnp.sum(gt.astype(F32) * ot, axis=0, keepdims=True)

    def far3(h):
        sf[...] = nn(pool[h, 1].reshape(NF * B, D), gt_s[...]).reshape(NF, B, T)
        for i in range(NF):
            df[i] = (ef[i].astype(F32) * (sf[i] - de_s[...])).astype(BF)
        dpool[h, 1] = nn(ef[...].reshape(NF * B, T), gs_s[...]).astype(BF).reshape(NF, B, D)
        dpool[h, 0] = (nn(df[...].reshape(NF * B, T), qb[h]) * SCALE).astype(BF).reshape(NF, B, D)

    def near3(h):
        dqt_s[...] = tn(pool[h, 0].reshape(NF * B, D), df[...].reshape(NF * B, T))
        dkw[h] = jnp.zeros((W, D), F32)
        dvw[h] = jnp.zeros((W, D), F32)
        for p in range(3):
            cols, r = pair_cols(p), pair_rows(p)
            e = en[p]
            dvw[h, r, :] += nn(e, gs_s[cols, :])
            dp = nn(vb[h, r, :], gt_s[:, cols])
            ds = (e.astype(F32) * (dp - de_s[:, cols])).astype(BF)
            dkw[h, r, :] += nn(ds, qb[h, cols, :]) * SCALE
            dqt_s[:, cols] += tn(kb[h, r, :], ds)
        back_s[0, h] = dkw[h, :EDGE, :].astype(BF)
        back_s[1, h] = dvw[h, :EDGE, :].astype(BF)
        dqb[h] = (dqt_s[...].T * SCALE).astype(BF)

    outs = ((ob, o_out), (dqb, dq_out), (dkb, dk_out), (dvb, dv_out))

    def o_start(n, h):
        src, dst = outs[n]
        place = dst.at[:, lanes(z, h)]
        for d in (2, 1, 3):
            to = (z + d) % Z
            part = src.at[h, pl.ds(pl.multiple_of(to * R, 64), R), :]
            remote(part, place, o_s.at[n, h], o_r.at[n, h], at(ctx, to)).start()
        part = src.at[h, pl.ds(pl.multiple_of(z * R, 64), R), :]
        pltpu.make_async_copy(part, place, o_r.at[n, h]).start()

    def sib_send(h):
        remote(dpool.at[h, 1 - c], sib_r.at[h], gs_sd.at[h], gs_rc.at[h], at(sib, z)).start()

    def g0(h):
        @pl.when(ctx > 0)
        def _():
            for n in range(2):
                remote(back_s.at[n, h], back_r.at[n, h], b_s.at[n, h], b_r.at[n, h], at(down, z)).start()

        o_start(1, h)

    def g1(h):
        done(sib_r.at[h], gs_rc.at[h])
        for i in range(NF):
            pair[h, i] = (dpool[h, c, i].astype(F32) + sib_r[h, i].astype(F32)).astype(BF)
        for d in (2, 1, 3):
            to = (x + d) % 4
            remote(pair.at[h, pl.ds(3 * to, 3)], x_r.at[h, d - 1], gx_s.at[h], gx_rc.at[h], at(xpeer(d), z)).start()

    def g2(h):
        done(x_r.at[h], gx_rc.at[h])
        tot = []
        for j in range(3):
            t = pair[h, 3 * x + j].astype(F32)
            for d in range(3):
                t = t + x_r[h, d, j].astype(F32)
            tot.append(t)
        for s in range(8):
            t = jnp.zeros((B, D), F32)
            for j in range(3):
                if 16 * j <= s * NB + 5 and s * NB <= 16 * j + 15:
                    t = jnp.where((phase + 16 * j) // NB == s, tot[j], t)
            ysl[h, s] = t.astype(BF)
        for d, other in row_moves:
            to = rowpeer(d, other)
            remote(ysl.at[h, to], y_r.at[h, me8], gy_s.at[h], gy_rc.at[h], at(x * 8 + to, z)).start()
        y_r[h, me8] = ysl[h, me8]

    def g3(h):
        done(y_r.at[h, :7], gy_rc.at[h])

        @pl.when(ctx < 31)
        def _():
            done(back_r.at[0, h], b_r.at[0, h])
            done(back_r.at[1, h], b_r.at[1, h])

        for n, (part, total, dst) in enumerate(
            ((y_r, dkw, dkb), (y_r, dvw, dvb))
        ):
            part = part[h, n].astype(F32) + part[h, 2 + n].astype(F32) + part[h, 4 + n].astype(F32) + part[h, 6 + n].astype(F32)
            for b in range(NB):
                r = slice(b * B, (b + 1) * B)
                t = total[h, EDGE + b * B:EDGE + (b + 1) * B, :] + jnp.where(own == b, part, 0.0)
                if b >= 3:
                    t = t + back_r[n, h, (b - 3) * B:(b - 2) * B, :].astype(F32)
                dst[h, r, :] = t.astype(BF)
        o_start(2, h)
        o_start(3, h)

    for h, which in ((0, KV), (1, KV), (2, KV), (0, QG), (3, KV), (1, QG), (2, QG), (3, QG)):
        a_start(h, which)
    masks()
    b_stage(0)
    b_stage(1)
    d_stage(0)
    b_stage(2)
    d_stage(1)
    e_stage(0)

    @pl.loop(0, H)
    def _(t):
        f_stage(t)
        near1(t)

        @pl.when(t == 0)
        def _():
            d_stage(2)

        @pl.when(t >= 1)
        def _():
            g1(t - 1)

        f2_stage(t)
        far1(t)

        @pl.when(t == 0)
        def _():
            b_stage(3)

        @pl.when(t + 1 < H)
        def _():
            e_stage(t + 1)

        pass2(t)
        o_start(0, t)

        @pl.when(t >= 2)
        def _():
            g2(t - 2)

        @pl.when(t >= 3)
        def _():
            g3(t - 3)

        far3(t)
        sib_send(t)

        @pl.when(t == 0)
        def _():
            d_stage(3)

        near3(t)
        g0(t)

    g1(H - 1)
    g3(H - 3)
    g2(H - 2)
    g3(H - 2)
    g2(H - 1)
    g3(H - 1)

    @pl.loop(0, H)
    def _(h):
        for n in range(4):
            done(qb.at[h, :3 * R, :], a_s.at[n, h])
            done(qb.at[h, :3 * R, :], o_s.at[n, h])
            done(qb.at[h], o_r.at[n, h])
        done(rows.at[h, :7], y1_s.at[h])
        done(pool.at[h, 0, :9], x1_s.at[h])
        done(pool.at[h, 0], s2_s.at[h])
        done(sib_r.at[h], gs_sd.at[h])
        done(x_r.at[h], gx_s.at[h])
        done(y_r.at[h, :7], gy_s.at[h])

        @pl.when(ctx < 31)
        def _():
            done(back_r.at[0, h], h_s.at[0, h])
            done(back_r.at[0, h], h_s.at[1, h])

        @pl.when(ctx > 0)
        def _():
            done(back_r.at[0, h], b_s.at[0, h])
            done(back_r.at[0, h], b_s.at[1, h])


def settle(*refs):
    src, dst, held, in_sem, out_sem = refs[:4], refs[4:8], refs[8], refs[9], refs[10]
    half = R // 2
    parts = [(n, slice(m * half, (m + 1) * half), 2 * n + m) for n in range(4) for m in range(2)]
    ins = [pltpu.make_async_copy(src[n].at[r], held.at[n, r], in_sem.at[i]) for n, r, i in parts]
    outs = [pltpu.make_async_copy(held.at[n, r], dst[n].at[r], out_sem.at[i]) for n, r, i in parts]
    for copy in ins:
        copy.start()
    for first, second in zip(ins, outs):
        first.wait()
        second.start()
    for copy in outs:
        copy.wait()


def finish(results):
    return pl.pallas_call(
        settle,
        out_shape=[jax.ShapeDtypeStruct((R, H * Z * D), BF)] * 4,
        in_specs=[pl.BlockSpec(memory_space=pl.ANY)] * 4,
        out_specs=[pl.BlockSpec(memory_space=pl.ANY)] * 4,
        scratch_shapes=[
            pltpu.VMEM((4, R, H * Z * D), BF),
            pltpu.SemaphoreType.DMA((8,)),
            pltpu.SemaphoreType.DMA((8,)),
        ],
        compiler_params=pltpu.CompilerParams(vmem_limit_bytes=58 * 1024 * 1024),
    )(*results)


def per_device(queries, keys, values, grad_out, pattern):
    vm = pltpu.VMEM
    dma = pltpu.SemaphoreType.DMA
    results = pl.pallas_call(
        kernel,
        out_shape=[jax.ShapeDtypeStruct((R, H * Z * D), BF)] * 4,
        in_specs=[pl.BlockSpec(memory_space=pl.ANY)] * 4 + [pl.BlockSpec(memory_space=pltpu.SMEM)],
        out_specs=[pl.BlockSpec(memory_space=pl.ANY)] * 4,
        scratch_shapes=[
            vm((H, W, D), BF), vm((H, W, D), BF), vm((H, T, D), BF), vm((H, T, D), BF),
            vm((H, B, D), BF), vm((H, 8, B, D), BF), vm((H, 2, NF, B, D), BF),
            vm((H, T, D), BF), vm((H, T, D), BF), vm((H, W, D), F32), vm((H, W, D), F32),
            vm((H, T, D), BF), vm((H, T, D), BF), vm((2, H, EDGE, D), BF), vm((2, H, EDGE, D), BF),
            vm((H, 2, NF, B, D), BF), vm((H, NF, B, D), BF), vm((H, NF, B, D), BF),
            vm((H, 3, 3, B, D), BF), vm((H, 8, B, D), BF), vm((H, 8, B, D), BF),
            vm((16, T), F32), vm((NF, B, T), F32), vm((3, 640, 256), F32), vm((NF, B, T), BF), vm((3, 640, 256), BF),
            vm((1, T), F32), vm((1, T), F32), vm((D, T), F32), vm((D, T), F32),
            vm((D, T), BF), vm((T, D), BF), vm((1, T), F32), vm((D, T), BF),
            vm((NF, B, T), BF), vm((3, 640, 256), F32),
            dma((4, H)), dma((4, H)), dma((2, H)), dma((2, H)), dma((H,)), dma((H,)), dma((H,)), dma((H,)),
            dma((H,)), dma((H,)),
            dma((4, H)), dma((4, H)), dma((H,)), dma((H,)), dma((H,)), dma((H,)), dma((H,)), dma((H,)),
            dma((2, H)), dma((2, H)),
        ],
        compiler_params=pltpu.CompilerParams(
            collective_id=0, has_side_effects=True, vmem_limit_bytes=58 * 1024 * 1024
        ),
    )(keys, values, queries, grad_out, pattern.T)
    return finish(results)


def solution(mesh):
    split = P(("ctx", "head"), None)
    return jax.shard_map(
        per_device, mesh=mesh, in_specs=(split,) * 4 + (P(),), out_specs=(split,) * 4, check_vma=False
    )
```
